32 devices in a mesh: dp: 8 (over y, x, core), blk: 4 (over z).
Axes of the slice: x: 2, y: 2, z: 4, core: 2. Of those that a mesh axis runs over, the one named last changes fastest.
Arguments:
- tokens: bfloat16 [32, 512, 768], P('dp', 'blk'), may hold values from -6 to 6
- row_kinds: int32 [32], P('dp'), may hold values from 0 to 1, as said below
- live_mask: int32 [32, 512], P('dp', 'blk'), may hold values from 0 to 1, as said below
- keep_flag: int32 [32], P('dp'), may hold values 0 or 1
- projection: bfloat16 [768, 2304], replicated, may hold values from -0.21875 to 0.21875
- proj_bias: bfloat16 [2, 768], replicated, may hold values from -3 to 3
- mixing: bfloat16 [768, 768], replicated, may hold values from -3.5 to 3.5
- mix_bias: bfloat16 [768], replicated, may hold values from -2 to 2
- attn_gain: bfloat16 [768], replicated, may hold values from 0.5 to 1.5
- attn_shift: bfloat16 [768], replicated, may hold values from -2 to 2
- expand: bfloat16 [768, 3072], replicated, may hold values from -0.21875 to 0.21875
- expand_bias: bfloat16 [3072], replicated, may hold values from -3 to 3
- contract: bfloat16 [3072, 768], replicated, may hold values from -0.109375 to 0.109375
- contract_bias: bfloat16 [768], replicated, may hold values from -2 to 2
- ffn_gain: bfloat16 [768], replicated, may hold values from 0.5 to 1.5
- ffn_shift: bfloat16 [768], replicated, may hold values from -2 to 2
- cotangent: bfloat16 [32, 512, 768], P('dp', 'blk'), may hold values from -6 to 6
Outputs:
- layer_out: bfloat16 [32, 512, 768], P('dp', 'blk')
- tokens_grad: float32 [32, 512, 768], P('dp', 'blk')
- projection_grad: float32 [768, 2304], replicated
- proj_bias_grad: float32 [2, 768], replicated
- mixing_grad: float32 [768, 768], replicated
- mix_bias_grad: float32 [768], replicated
- attn_gain_grad: float32 [768], replicated
- attn_shift_grad: float32 [768], replicated
- expand_grad: float32 [768, 3072], replicated
- expand_bias_grad: float32 [3072], replicated
- contract_grad: float32 [3072, 768], replicated
- contract_bias_grad: float32 [768], replicated
- ffn_gain_grad: float32 [768], replicated
- ffn_shift_grad: float32 [768], replicated
The draws below stay inside these ranges and needn't reach their ends.
Inputs may be any that keep to these rules, and one draw needn't show every extreme that they name: `row_kinds`: in each aligned group of 4 rows at least one row has kind 1. `live_mask`: each row is live on a prefix of its positions; fewer than 128 last positions of a row are padding.
All inputs are finite; a program needn't handle non-finite values. No bound on the sum of `keep_flag` on one device may be relied on, other than what follows from the above.
Results may differ from the reference program's by a relative error of at most 0.014.
Values may be sent and summed in bfloat16 or wider, within the bound.
A program may use at most 192 MiB of HBM per device.

```python
import jax
import jax.numpy as jnp
from jax import lax

D = 768
HEADS = 12
HEAD_DIM = 64
FF = 3072
ROWS_DEV = 4
ROW_LEN = 512
ROWS = 32
DOC_SHORT = 128


def draw_row_kinds(key, part):
    key = jax.random.fold_in(key, 11)
    first_key, second_key = jax.random.split(key)
    groups = ROWS // ROWS_DEV
    chosen = jax.random.randint(first_key, (groups,), 0, ROWS_DEV)
    others = jax.random.randint(second_key, (ROWS,), 0, 2)
    within = jnp.arange(ROWS) % ROWS_DEV
    return jnp.where(within == jnp.repeat(chosen, ROWS_DEV), 1, others).astype(jnp.int32)


def draw_live_mask(key, part):
    key = jax.random.fold_in(key, 23)
    padding = jax.random.randint(key, (ROWS, 1), 0, DOC_SHORT)
    positions = jnp.arange(ROW_LEN)[None, :]
    return (positions < ROW_LEN - padding).astype(jnp.int32)


def touch_ends(entries, own_key, low, top_value):
    longest = entries.shape.index(max(entries.shape))
    spots = []
    for shift in (0, 1):
        where = [jax.random.randint(jax.random.fold_in(own_key, axis), (), 0, length) for axis, length in enumerate(entries.shape)]
        where[longest] = (where[longest] + shift) % entries.shape[longest]
        spots.append(tuple(where))
    return entries.at[spots[0]].set(low).at[spots[1]].set(top_value)


def block_levels(rng, shape, cuts, smallest, high):
    level, own = 1.0, jax.random.fold_in(rng, 6)
    for dim, blocks in cuts:
        steps = jnp.exp(jax.random.uniform(jax.random.fold_in(own, dim), (blocks,), jnp.float32, smallest / len(cuts), high / len(cuts)))
        level = level * jnp.repeat(steps, shape[dim] // blocks).reshape([-1 if axis == dim else 1 for axis in range(len(shape))])
    return level


def centred(stream_key, dims, spread, limit, shards=(), held_as=jnp.bfloat16):
    values = spread * jax.random.normal(stream_key, dims, jnp.float32)
    if shards:
        values = values * block_levels(stream_key, dims, shards, -0.22, 0.18)
    return jnp.clip(values, -limit, limit).astype(held_as)


def setup_inputs(seed: int = 0) -> dict:
    keys = jax.random.split(jax.random.key(seed), 18)
    tokens = centred(keys[0], (ROWS, ROW_LEN, D), 1.0, 6.0, ((0, 8), (1, 4)))
    row_kinds = draw_row_kinds(jax.random.fold_in(keys[17], 71), 0)
    live_mask = draw_live_mask(jax.random.fold_in(keys[17], 71), 0)
    keep_flag = touch_ends((jax.random.randint(keys[3], (ROWS,), 0, 4) < 3).astype(jnp.int32), jax.random.fold_in(keys[3], 1), 0, 1)
    projection = centred(keys[4], (D, 3 * D), D ** -0.5, 0.21875)
    proj_bias = centred(keys[5], (2, D), 0.5, 3.0)
    mixing = centred(keys[6], (D, D), (max(D // 256, 1)) ** -0.5, 3.5)
    mix_bias = centred(keys[7], (D,), 0.3, 2.0)
    attn_gain = jnp.clip(1.0 + 0.1 * jax.random.normal(keys[8], (D,), jnp.float32), 0.5, 1.5).astype(jnp.bfloat16)
    attn_shift = centred(keys[9], (D,), 0.3, 2.0)
    expand = centred(keys[10], (D, FF), D ** -0.5, 0.21875)
    expand_bias = centred(keys[11], (FF,), 0.5, 3.0)
    contract = centred(keys[12], (FF, D), FF ** -0.5, 0.109375)
    contract_bias = centred(keys[13], (D,), 0.3, 2.0)
    ffn_gain = jnp.clip(1.0 + 0.1 * jax.random.normal(keys[14], (D,), jnp.float32), 0.5, 1.5).astype(jnp.bfloat16)
    ffn_shift = centred(keys[15], (D,), 0.3, 2.0)
    cotangent = centred(keys[16], (ROWS, ROW_LEN, D), 1.0, 6.0, ((0, 8), (1, 4)))
    return {"tokens": tokens, "row_kinds": row_kinds, "live_mask": live_mask, "keep_flag": keep_flag, "projection": projection, "proj_bias": proj_bias, "mixing": mixing, "mix_bias": mix_bias, "attn_gain": attn_gain, "attn_shift": attn_shift, "expand": expand, "expand_bias": expand_bias, "contract": contract, "contract_bias": contract_bias, "ffn_gain": ffn_gain, "ffn_shift": ffn_shift, "cotangent": cotangent}


@jax.custom_vjp
def low(v):
    return lax.optimization_barrier(v.astype(jnp.bfloat16)).astype(jnp.float32)

@jax.custom_vjp
def low_back(v):
    return v

def low_keep(v):
    return (low(v), None)

def low_pass(kept, grad):
    return (grad,)

def back_keep(v):
    return (v, None)

def back_low(kept, grad):
    return (low(grad),)
low.defvjp(low_keep, low_pass)
low_back.defvjp(back_keep, back_low)
highest = lax.Precision.HIGHEST
norm_eps = 1e-05

def layer_norm(hidden, gain_vec, shift_vec):
    row_mean = lax.optimization_barrier(jnp.mean(hidden, axis=-1, keepdims=True))
    centered = hidden - row_mean
    variance = lax.optimization_barrier(jnp.mean(centered * centered, axis=-1, keepdims=True))
    return centered * lax.rsqrt(variance + norm_eps) * gain_vec + shift_vec

def rounded(value_in):
    return low_back(low(value_in))

def row_layer(params, row_tokens, row_kind, row_live, row_keep):
    projection, proj_bias, mixing, mix_bias, attn_gain, attn_shift, expand, expand_bias, contract, contract_bias, ffn_gain, ffn_shift = params
    length = row_tokens.shape[0]
    projected = jnp.dot(row_tokens, projection, precision=highest)
    queries = rounded(projected[:, :D] + proj_bias[0])
    key_rows = rounded(projected[:, D:2 * D])
    value_rows = rounded(projected[:, 2 * D:] + proj_bias[1])
    positions = jnp.arange(length, dtype=jnp.int32)
    doc_len = jnp.where(row_kind == 0, DOC_SHORT, length).astype(jnp.int32)
    segment = positions // doc_len
    allowed = (segment[:, None] == segment[None, :]) & (row_live[None, :] > 0)
    query_heads = queries.reshape(length, HEADS, HEAD_DIM)
    key_heads = key_rows.reshape(length, HEADS, HEAD_DIM)
    value_heads = value_rows.reshape(length, HEADS, HEAD_DIM)
    scores = jnp.einsum('qhd,khd->hqk', query_heads, key_heads, precision=highest) * HEAD_DIM ** (-0.5)
    scores = low_back(jnp.where(allowed[None], scores, -1000000000.0))
    soft_probs = jax.nn.softmax(scores, axis=-1)
    attended = jnp.einsum('hqk,khd->qhd', low(soft_probs), value_heads, precision=highest)
    attended = rounded(attended.reshape(length, D))
    attn_out = low_back(jnp.dot(attended, mixing, precision=highest) + mix_bias)
    normed = layer_norm(row_tokens + attn_out, attn_gain, attn_shift)
    pre_act = low_back(jnp.dot(low(normed), expand, precision=highest) + expand_bias)
    activated = low(jax.nn.gelu(pre_act, approximate=False))
    ffn_out = low_back(jnp.dot(activated, contract, precision=highest) + contract_bias)
    normed_two = layer_norm(normed + ffn_out, ffn_gain, ffn_shift)
    return jnp.where(row_keep > 0, normed_two, row_tokens)

def reference(tokens, row_kinds, live_mask, keep_flag, projection, proj_bias, mixing, mix_bias, attn_gain, attn_shift, expand, expand_bias, contract, contract_bias, ffn_gain, ffn_shift, cotangent):
    params = tuple((weight_in.astype(jnp.float32) for weight_in in (projection, proj_bias, mixing, mix_bias, attn_gain, attn_shift, expand, expand_bias, contract, contract_bias, ffn_gain, ffn_shift)))
    inputs = tokens.astype(jnp.float32)

    def forward(params_in, tokens_in):

        def per_row(bundle):
            return jax.checkpoint(row_layer)(params_in, bundle[0], bundle[1], bundle[2], bundle[3])
        return lax.map(per_row, (tokens_in, row_kinds, live_mask, keep_flag))
    layer_out, pull_back = jax.vjp(forward, params, inputs)
    param_grads, tokens_grad = pull_back(cotangent.astype(jnp.float32))
    return (layer_out.astype(jnp.bfloat16), tokens_grad, param_grads[0], param_grads[1], param_grads[2], param_grads[3], param_grads[4], param_grads[5], param_grads[6], param_grads[7], param_grads[8], param_grads[9], param_grads[10], param_grads[11])
```

```python
import functools
import jax
import jax.numpy as jnp
from jax import lax
from jax.experimental import pallas as pl
from jax.experimental.pallas import tpu as pltpu
from jax.sharding import PartitionSpec as P

D = 768
HEADS = 12
HEAD_DIM = 64
DOC_SHORT = 128
MESH = pl.DeviceIdType.MESH
norm_eps = 1e-05
NEG = -1e9
F32, B16 = jnp.float32, jnp.bfloat16
NN = (((1,), (0,)), ((), ()))
NT = (((1,), (1,)), ((), ()))
TN = (((0,), (0,)), ((), ()))
def dot(a, b, dims=NN):
    return lax.dot_general(a, b, dims, preferred_element_type=F32)

def fwd_kernel(q, k, v, bias, att, probs):
    for h in range(2):
        s = slice(h * HEAD_DIM, (h + 1) * HEAD_DIM)
        scores = dot(q[:, s] * jnp.asarray(HEAD_DIM ** -0.5, B16), k[:, s], NT) + bias[...]
        top = jnp.max(scores, axis=1, keepdims=True)
        e = jnp.exp(scores - top)
        p = (e * (1.0 / jnp.sum(e, axis=1, keepdims=True))).astype(B16)
        probs[h] = p
        att[:, s] = dot(p, v[:, s]).astype(B16)

def attend(qkv, bias):
    T = qkv.shape[0]
    W = 2 * HEAD_DIM
    G = HEADS // 2
    col = lambda off: pl.BlockSpec((T, W), lambda i: (0, off + i))
    return pl.pallas_call(fwd_kernel, grid=(G,),
        in_specs=[col(0), col(G), col(2 * G), pl.BlockSpec((T, T), lambda i: (0, 0))],
        out_specs=[col(0), pl.BlockSpec((2, T, T), lambda i: (i, 0, 0))],
        out_shape=[jax.ShapeDtypeStruct((T, D), B16), jax.ShapeDtypeStruct((HEADS, T, T), B16)],
        compiler_params=pltpu.CompilerParams(vmem_limit_bytes=48 * 2**20),
        cost_estimate=pl.CostEstimate(flops=4 * T * T * D * 4, bytes_accessed=20 * 2**20, transcendentals=HEADS * T * T),
        name="attend")(qkv, qkv, qkv, bias)

def bwd_kernel(q, k, v, probs, da, dq, dk, dv):
    scale = HEAD_DIM ** -0.5
    for h in range(2):
        s = slice(h * HEAD_DIM, (h + 1) * HEAD_DIM)
        dah = da[:, s]
        p = probs[h]
        dp = dot(dah, v[:, s], NT)
        pf = p.astype(F32)
        delta = jnp.sum(pf * dp, axis=1, keepdims=True)
        ds = (pf * (dp - delta)).astype(B16)
        dq[:, s] = (dot(ds, k[:, s]) * scale).astype(B16)
        dk[:, s] = (dot(q[:, s], ds, TN) * scale).T.astype(B16)
        dv[:, s] = dot(dah, p, TN).T.astype(B16)

def attend_back(qkv, probs, da):
    T = qkv.shape[0]
    W = 2 * HEAD_DIM
    G = HEADS // 2
    col = lambda off: pl.BlockSpec((T, W), lambda i: (0, off + i))
    return pl.pallas_call(bwd_kernel, grid=(G,),
        in_specs=[col(0), col(G), col(2 * G), pl.BlockSpec((2, T, T), lambda i: (i, 0, 0)), col(0)],
        out_specs=[col(0)] * 3,
        out_shape=[jax.ShapeDtypeStruct((T, D), B16)] * 3,
        compiler_params=pltpu.CompilerParams(vmem_limit_bytes=48 * 2**20),
        cost_estimate=pl.CostEstimate(flops=8 * T * T * D * 4, bytes_accessed=20 * 2**20, transcendentals=0),
        name="attend_back")(qkv, qkv, qkv, probs, da)


CR, CC = 384, 768
HR, HC = CR // 2, CC // 2
SR = HR // 4
N = 24
KINDS = 12
OFF = [0, 1, 4, 6, 8, 10, 12, 14, 16, 18, 21, 22]
CORE, FIRST, ZA, ZB, ZC, LAST, GR, GL, GF, GE, AGF, AGC = range(KINDS)

def grads_kernel(act, d_ffn, low, d_pre, att, d_att, tok, d_proj, small, g_out, small_out,
           part, r0, r1, za, zb, zc, ry, fin, sm, smr, ssem, rsem, lsem, smss, smrs):
    dp, z = lax.axis_index("dp"), lax.axis_index("blk")
    c, x, y = dp % 2, (dp // 2) % 2, (dp // 4) % 2
    d_core = (dp + 1 - 2 * c, z)
    d_x = (dp + 2 - 4 * x, z)
    d_y = (dp + 4 - 8 * y, z)
    right, left = (dp, jnp.minimum(z + 1, 3)), (dp, jnp.maximum(z - 1, 0))
    is0, is1, is2, is3 = z == 0, z == 1, z == 2, z == 3
    end, mid = (z == 0) | (z == 3), (z == 1) | (z == 2)

    barrier = pltpu.get_barrier_semaphore()
    for d in (d_core, d_x, d_y):
        pl.semaphore_signal(barrier, inc=1, device_id=d, device_id_type=MESH)
    @pl.when(z < 3)
    def _():
        pl.semaphore_signal(barrier, inc=1, device_id=right, device_id_type=MESH)
    @pl.when(z > 0)
    def _():
        pl.semaphore_signal(barrier, inc=1, device_id=left, device_id_type=MESH)
    pl.semaphore_wait(barrier, jnp.where(end, 4, 5))

    def cp(kind, k, src, dst, dev):
        return pltpu.make_async_remote_copy(src_ref=src, dst_ref=dst, send_sem=ssem.at[kind, k],
            recv_sem=rsem.at[kind, k], device_id=dev, device_id_type=MESH)

    def ctx(k):
        par = k % 2
        f = x * (1 - par) + y * par
        d_first = (dp + (1 - par) * (2 - 4 * x) + par * (4 - 8 * y), z)
        d_last = (dp + par * (2 - 4 * x) + (1 - par) * (4 - 8 * y), z)
        return f, d_first, d_last

    def rows(start, n):
        return pl.ds(pl.multiple_of(start, 16), n)
    def cols(start, n):
        return pl.ds(pl.multiple_of(start, 128), n)
    keep = rows(c * HR, HR)
    give = rows((1 - c) * HR, HR)

    def c_core(k):
        return cp(CORE, k, part.at[k % 2, give], r0.at[k], d_core)
    def c_first(k):
        f, d_first, _ = ctx(k)
        return cp(FIRST, k, r0.at[k, :, cols((1 - f) * HC, HC)], r1.at[k], d_first)
    def c_za(k):
        src = r1.at[k, rows(jnp.where(is0, SR, 0), 3 * SR)]
        return cp(ZA, k, src, za.at[k], (dp, jnp.where(is0, 1, 2)))
    def c_zb(k):
        src = r1.at[k, rows(jnp.where(is1, 2 * SR, 0), 2 * SR)]
        return cp(ZB, k, src, zb.at[k], (dp, jnp.where(is1, 2, 1)))
    def c_zc(k):
        src = r1.at[k, rows(jnp.where(is1, 0, 3 * SR), SR)]
        return cp(ZC, k, src, zc.at[k], (dp, jnp.where(is1, 0, 3)))
    def c_last(k):
        _, _, d_last = ctx(k)
        return cp(LAST, k, r1.at[k, rows(z * SR, SR)], ry.at[k], d_last)
    def place(k, shard, n=1):
        f, _, _ = ctx(k)
        return g_out.at[k, rows(c * HR + shard * SR, n * SR), cols(f * HC, HC)]
    def c_gr(k):
        return cp(GR, k, fin.at[k], place(k, z), right)
    def c_gl(k):
        return cp(GL, k, fin.at[k], place(k, z), left)
    def c_own(k):
        return pltpu.make_async_copy(fin.at[k], place(k, z), lsem.at[k])
    def c_gf(k):
        s = jnp.where(is1, 0, 3)
        return cp(GF, k, place(k, s), place(k, s), (dp, jnp.where(is1, 2, 1)))
    def c_ge(k):
        s = jnp.where(is1, 2, 0)
        return cp(GE, k, place(k, s, 2), place(k, s, 2), (dp, jnp.where(is1, 0, 3)))
    def c_agf(k):
        f, d_first, _ = ctx(k)
        blk = g_out.at[k, keep, cols(f * HC, HC)]
        return cp(AGF, k, blk, blk, d_first)
    def c_agc(k):
        blk = g_out.at[k, keep]
        return cp(AGC, k, blk, blk, d_core)

    def add(a, b):
        return (a.astype(jnp.float32) + b.astype(jnp.float32)).astype(jnp.bfloat16)

    def produce(k):
        def dot(l, lc, r, rc):
            return lax.dot_general(l[:, cols(lc * CR, CR)], r[:, cols(rc * CC, CC)], (((0,), (0,)), ((), ())),
                                   preferred_element_type=jnp.float32).astype(jnp.bfloat16)
        @pl.when(k < 8)
        def _():
            part[k % 2] = dot(act, k, d_ffn, 0)
        @pl.when((k >= 8) & (k < 16))
        def _():
            j = k - 8
            part[k % 2] = dot(low, j // 4, d_pre, j % 4)
        @pl.when((k >= 16) & (k < 18))
        def _():
            part[k % 2] = dot(att, k - 16, d_att, 0)
        @pl.when(k >= 18)
        def _():
            j = k - 18
            part[k % 2] = dot(tok, j // 3, d_proj, j % 3)

    def stage(s, k):
        if s == 0:
            @pl.when(k >= 2)
            def _(): c_core(k - 2).wait_send()
            produce(k)
            c_core(k).start()
        elif s == 1:
            c_core(k).wait_recv()
            r0[k] = add(r0[k], part[k % 2, keep])
            c_first(k).start()
        elif s == 2:
            f, _, _ = ctx(k)
            c_first(k).wait_recv()
            r1[k] = add(r1[k], r0[k, :, cols(f * HC, HC)])
            @pl.when(end)
            def _(): c_za(k).start()
        elif s == 3:
            @pl.when(mid)
            def _():
                c_za(k).wait_recv()
                own = rows(jnp.where(is1, SR, 0), 3 * SR)
                r1[k, own] = add(r1[k, own], za[k])
                c_zb(k).start()
        elif s == 4:
            @pl.when(mid)
            def _():
                c_zb(k).wait_recv()
                own = rows(jnp.where(is1, 0, 2 * SR), 2 * SR)
                r1[k, own] = add(r1[k, own], zb[k])
                c_zc(k).start()
        elif s == 5:
            @pl.when(end)
            def _():
                c_zc(k).wait_recv()
                own = rows(z * SR, SR)
                r1[k, own] = add(r1[k, own], zc[k])
            c_last(k).start()
        elif s == 6:
            c_last(k).wait_recv()
            fin[k] = add(r1[k, rows(z * SR, SR)], ry[k])
            c_own(k).start()
            @pl.when(z < 3)
            def _(): c_gr(k).start()
            @pl.when(z > 0)
            def _(): c_gl(k).start()
        elif s == 7:
            @pl.when(is1)
            def _(): c_gr(k).wait_recv()
            @pl.when(is2)
            def _(): c_gl(k).wait_recv()
            @pl.when(mid)
            def _(): c_gf(k).start()
        elif s == 8:
            @pl.when(is1)
            def _(): c_gl(k).wait_recv()
            @pl.when(is2)
            def _(): c_gr(k).wait_recv()
            @pl.when(mid)
            def _():
                c_gf(k).wait_recv()
                c_ge(k).start()
        elif s == 9:
            @pl.when(is0)
            def _(): c_gl(k).wait_recv()
            @pl.when(is3)
            def _(): c_gr(k).wait_recv()
            @pl.when(end)
            def _(): c_ge(k).wait_recv()
            c_own(k).wait()
            c_agf(k).start()
        elif s == 10:
            c_agf(k).wait_recv()
            c_agc(k).start()
        elif s == 11:
            c_agc(k).wait_recv()
            c_first(k).wait_send()
            c_last(k).wait_send()
            @pl.when(end)
            def _(): c_za(k).wait_send()
            @pl.when(mid)
            def _():
                c_zb(k).wait_send()
                c_zc(k).wait_send()
                c_gf(k).wait_send()
                c_ge(k).wait_send()
            @pl.when(z < 3)
            def _(): c_gr(k).wait_send()
            @pl.when(z > 0)
            def _(): c_gl(k).wait_send()
            c_agf(k).wait_send()
            c_agc(k).wait_send()

    def s_copy(i):
        dev = (d_core, d_x, d_y, (dp, jnp.where(is0, 1, 2)), (dp, jnp.where(is1, 2, 1)), (dp, jnp.where(is1, 0, 3)))[i]
        return pltpu.make_async_remote_copy(src_ref=sm.at[i], dst_ref=smr.at[i], send_sem=smss.at[i], recv_sem=smrs.at[i],
            device_id=dev, device_id_type=MESH)
    sm[0] = small[...]
    def s_step(i):
        if i > 0:
            sends = (None, None, None, end, mid, mid)[i - 1]
            gets = (None, None, None, mid, mid, end)[i - 1]
            def get():
                s_copy(i - 1).wait_recv()
                if i == 6:
                    sm[i] = smr[i - 1]
                else:
                    sm[i] = sm[i - 1] + smr[i - 1]
            if gets is None:
                get()
            else:
                pl.when(gets)(get)
                @pl.when(jnp.logical_not(gets))
                def _(): sm[i] = sm[i - 1]
        if i < 6:
            sends = (None, None, None, end, mid, mid)[i]
            if sends is None:
                s_copy(i).start()
            else:
                pl.when(sends)(lambda: s_copy(i).start())

    def tick(t, _):
        for s in range(len(OFF) - 1, -1, -1):
            k = t - OFF[s]
            @pl.when((k >= 0) & (k < N))
            def _():
                stage(s, k)
        for i in range(7):
            @pl.when(t == N + i)
            def _():
                s_step(i)
        return 0
    lax.fori_loop(0, N + OFF[-1], tick, 0)
    for i in range(6):
        sends = (None, None, None, end, mid, mid)[i]
        if sends is None:
            s_copy(i).wait_send()
        else:
            pl.when(sends)(lambda: s_copy(i).wait_send())
    @pl.when(mid)
    def _(): small_out[...] = sm[5]
    @pl.when(end)
    def _(): small_out[...] = sm[6]
    for k in (N - 2, N - 1):
        c_core(k).wait_send()

def sum_grads(act, d_ffn, low, d_pre, att, d_att, tok, d_proj, small):
    B = jnp.bfloat16
    V = pl.BlockSpec(memory_space=pltpu.VMEM)
    return pl.pallas_call(grads_kernel,
        out_shape=[jax.ShapeDtypeStruct((N, CR, CC), B), jax.ShapeDtypeStruct(small.shape, jnp.float32)],
        in_specs=[V] * 9,
        out_specs=[pl.BlockSpec(memory_space=pltpu.HBM), V],
        scratch_shapes=[
            pltpu.VMEM((2, CR, CC), B), pltpu.VMEM((N, HR, CC), B), pltpu.VMEM((N, HR, HC), B),
            pltpu.VMEM((N, 3 * SR, HC), B), pltpu.VMEM((N, 2 * SR, HC), B), pltpu.VMEM((N, SR, HC), B),
            pltpu.VMEM((N, SR, HC), B), pltpu.VMEM((N, SR, HC), B),
            pltpu.VMEM((7,) + small.shape, jnp.float32), pltpu.VMEM((6,) + small.shape, jnp.float32),
            pltpu.SemaphoreType.DMA((KINDS, N)), pltpu.SemaphoreType.DMA((KINDS, N)), pltpu.SemaphoreType.DMA((N,)),
            pltpu.SemaphoreType.DMA((6,)), pltpu.SemaphoreType.DMA((6,)),
        ],
        compiler_params=pltpu.CompilerParams(collective_id=0, has_side_effects=True, vmem_limit_bytes=60 * 2**20),
        name="grads",
    )(act, d_ffn, low, d_pre, att, d_att, tok, d_proj, small)


def deal(blocks):
    z = lax.axis_index("blk")
    n = blocks.shape[0]
    out = jnp.zeros_like(blocks)
    for m in range(n):
        piece = lax.dynamic_index_in_dim(blocks, z ^ m, 0)
        if m:
            piece = lax.ppermute(piece, "blk", [(i, i ^ m) for i in range(n)])
        out = lax.dynamic_update_slice(out, piece, (z ^ m,) + (0,) * (blocks.ndim - 1))
    return out


def layer_norm(hidden, gain_vec, shift_vec):
    row_mean = jnp.mean(hidden, axis=-1, keepdims=True)
    centered = hidden - row_mean
    variance = jnp.mean(centered * centered, axis=-1, keepdims=True)
    return centered * lax.rsqrt(variance + norm_eps) * gain_vec + shift_vec


def local(tokens, row_kinds, live_mask, keep_flag, projection, proj_bias, mixing, mix_bias, attn_gain, attn_shift,
          expand, expand_bias, contract, contract_bias, ffn_gain, ffn_shift, cotangent):
    row_count, block_len, _ = tokens.shape
    blocks = lax.axis_size("blk")
    length = block_len * blocks
    z = lax.axis_index("blk")
    f32 = lambda a: a.astype(F32)
    row = deal(tokens).reshape(length, D)
    live = deal(live_mask[:, None]).reshape(length)
    cot = deal(cotangent).reshape(length, D)
    kind = lax.dynamic_index_in_dim(row_kinds, z, 0, False)
    keep = lax.dynamic_index_in_dim(keep_flag, z, 0, False) > 0

    seg = jnp.arange(length, dtype=jnp.int32) // jnp.where(kind == 0, DOC_SHORT, length)
    allowed = (seg[:, None] == seg[None, :]) & (live[None, :] > 0)
    bias = jnp.where(allowed, 0.0, NEG).astype(F32)
    qkv_bias = jnp.concatenate([f32(proj_bias[0]), jnp.zeros((D,), F32), f32(proj_bias[1])])
    qkv = (dot(row, projection) + qkv_bias).astype(B16)
    attended, probs = attend(qkv, bias)

    attn_out = dot(attended, mixing) + f32(mix_bias)
    normed, norm_one_back = jax.vjp(layer_norm, f32(row) + attn_out, f32(attn_gain), f32(attn_shift))
    normed_low = normed.astype(B16)
    pre_act = dot(normed_low, expand) + f32(expand_bias)
    gelu_value, gelu_back = jax.vjp(functools.partial(jax.nn.gelu, approximate=False), pre_act)
    activated = gelu_value.astype(B16)
    ffn_out = dot(activated, contract) + f32(contract_bias)
    normed_two, norm_two_back = jax.vjp(layer_norm, normed + ffn_out, f32(ffn_gain), f32(ffn_shift))
    layer_out = jnp.where(keep, normed_two, f32(row)).astype(B16)
    layer_out = deal(layer_out.reshape(blocks, block_len, D))

    grad_two = jnp.where(keep, f32(cot), 0.0)
    d_resid_two, ffn_gain_grad, ffn_shift_grad = norm_two_back(grad_two)
    d_ffn = d_resid_two.astype(B16)
    d_act = dot(d_ffn, contract, NT)
    d_pre = gelu_back(d_act)[0].astype(B16)
    d_normed = d_resid_two + dot(d_pre, expand, NT)
    d_resid_one, attn_gain_grad, attn_shift_grad = norm_one_back(d_normed)
    d_attn = d_resid_one.astype(B16)
    d_attended = dot(d_attn, mixing, NT).astype(B16)
    d_proj = jnp.concatenate(attend_back(qkv, probs, d_attended), axis=1)
    d_tokens = d_resid_one + dot(d_proj, projection, NT)
    tokens_grad = jnp.where(keep, d_tokens, f32(cot)).astype(B16)
    tokens_grad = deal(tokens_grad.reshape(blocks, block_len, D)).astype(F32)

    total = lambda a: jnp.sum(f32(a), axis=0)
    small = jnp.concatenate([total(d_proj[:, :D]), total(d_proj[:, 2 * D:]), total(d_attn), attn_gain_grad, attn_shift_grad,
        total(d_pre), total(d_ffn), ffn_gain_grad, ffn_shift_grad, jnp.zeros((4 * D,), F32)]).reshape(16, D)
    g, small = sum_grads(activated, d_ffn, normed_low, d_pre, attended, d_attn, row, d_proj, small)
    groups = lax.axis_size("dp") // 8
    if groups > 1:
        index = [[i + 8 * j for j in range(groups)] for i in range(8)]
        g, small = lax.psum((g, small), "dp", axis_index_groups=index)
    g = f32(g)
    contract_grad = g[:8].reshape(8 * CR, D)
    expand_grad = g[8:16].reshape(2, 4, CR, CC).transpose(0, 2, 1, 3).reshape(D, 4 * CC)
    mixing_grad = g[16:18].reshape(D, D)
    projection_grad = g[18:].reshape(2, 3, CR, CC).transpose(0, 2, 1, 3).reshape(D, 3 * D)
    return (layer_out, tokens_grad, projection_grad, small[:2], mixing_grad, small[2], small[3], small[4], expand_grad,
            small[5:9].reshape(-1), contract_grad, small[9], small[10], small[11])


def solution(mesh):
    data = P("dp", "blk", None)
    in_specs = (data, P("dp"), P("dp", "blk"), P("dp")) + (P(),) * 12 + (data,)
    out_specs = (data, data) + (P(),) * 12
    return jax.shard_map(local, mesh=mesh, in_specs=in_specs, out_specs=out_specs, check_vma=False)
```

```python
import functools
import jax
import jax.numpy as jnp
from jax import lax
from jax.experimental import pallas as pl
from jax.experimental.pallas import tpu as pltpu
from jax.sharding import PartitionSpec as P

D = 768
HEADS = 12
HEAD_DIM = 64
DOC_SHORT = 128
MESH = pl.DeviceIdType.MESH
norm_eps = 1e-05
NEG = -1e9
F32, B16 = jnp.float32, jnp.bfloat16
NN = (((1,), (0,)), ((), ()))
NT = (((1,), (1,)), ((), ()))
TN = (((0,), (0,)), ((), ()))
def dot(a, b, dims=NN):
    return lax.dot_general(a, b, dims, preferred_element_type=F32)

def fwd_kernel(q, k, v, bias, att, probs):
    for h in range(2):
        s = slice(h * HEAD_DIM, (h + 1) * HEAD_DIM)
        scores = dot(q[:, s] * jnp.asarray(HEAD_DIM ** -0.5, B16), k[:, s], NT) + bias[...]
        top = jnp.max(scores, axis=1, keepdims=True)
        e = jnp.exp(scores - top)
        p = (e * (1.0 / jnp.sum(e, axis=1, keepdims=True))).astype(B16)
        probs[h] = p
        att[:, s] = dot(p, v[:, s]).astype(B16)

def attend(qkv, bias):
    T = qkv.shape[0]
    W = 2 * HEAD_DIM
    G = HEADS // 2
    col = lambda off: pl.BlockSpec((T, W), lambda i: (0, off + i))
    return pl.pallas_call(fwd_kernel, grid=(G,),
        in_specs=[col(0), col(G), col(2 * G), pl.BlockSpec((T, T), lambda i: (0, 0))],
        out_specs=[col(0), pl.BlockSpec((2, T, T), lambda i: (i, 0, 0))],
        out_shape=[jax.ShapeDtypeStruct((T, D), B16), jax.ShapeDtypeStruct((HEADS, T, T), B16)],
        compiler_params=pltpu.CompilerParams(vmem_limit_bytes=48 * 2**20),
        cost_estimate=pl.CostEstimate(flops=4 * T * T * D * 4, bytes_accessed=20 * 2**20, transcendentals=HEADS * T * T),
        name="attend")(qkv, qkv, qkv, bias)

def bwd_kernel(q, k, v, probs, da, dq, dk, dv):
    scale = HEAD_DIM ** -0.5
    for h in range(2):
        s = slice(h * HEAD_DIM, (h + 1) * HEAD_DIM)
        dah = da[:, s]
        p = probs[h]
        dp = dot(dah, v[:, s], NT)
        pf = p.astype(F32)
        delta = jnp.sum(pf * dp, axis=1, keepdims=True)
        ds = (pf * (dp - delta)).astype(B16)
        dq[:, s] = (dot(ds, k[:, s]) * scale).astype(B16)
        dk[:, s] = (dot(q[:, s], ds, TN) * scale).T.astype(B16)
        dv[:, s] = dot(dah, p, TN).T.astype(B16)

def attend_back(qkv, probs, da):
    T = qkv.shape[0]
    W = 2 * HEAD_DIM
    G = HEADS // 2
    col = lambda off: pl.BlockSpec((T, W), lambda i: (0, off + i))
    return pl.pallas_call(bwd_kernel, grid=(G,),
        in_specs=[col(0), col(G), col(2 * G), pl.BlockSpec((2, T, T), lambda i: (i, 0, 0)), col(0)],
        out_specs=[col(0)] * 3,
        out_shape=[jax.ShapeDtypeStruct((T, D), B16)] * 3,
        compiler_params=pltpu.CompilerParams(vmem_limit_bytes=48 * 2**20),
        cost_estimate=pl.CostEstimate(flops=8 * T * T * D * 4, bytes_accessed=20 * 2**20, transcendentals=0),
        name="attend_back")(qkv, qkv, qkv, probs, da)


CR, CC = 384, 768
HR, HC = CR // 2, CC // 2
SR = HR // 4
N = 24
KINDS = 12
OFF = [0, 1, 4, 6, 8, 10, 12, 14, 16, 18, 21, 22]
CORE, FIRST, ZA, ZB, ZC, LAST, GR, GL, GF, GE, AGF, AGC = range(KINDS)

def grads_kernel(act, d_ffn, low, d_pre, att, d_att, tok, d_proj, small, g_out, small_out,
           part, r0, r1, za, zb, zc, ry, fin, sm, smr, ssem, rsem, lsem, smss, smrs):
    dp, z = lax.axis_index("dp"), lax.axis_index("blk")
    c, x, y = dp % 2, (dp // 2) % 2, (dp // 4) % 2
    d_core = (dp + 1 - 2 * c, z)
    d_x = (dp + 2 - 4 * x, z)
    d_y = (dp + 4 - 8 * y, z)
    right, left = (dp, jnp.minimum(z + 1, 3)), (dp, jnp.maximum(z - 1, 0))
    is0, is1, is2, is3 = z == 0, z == 1, z == 2, z == 3
    end, mid = (z == 0) | (z == 3), (z == 1) | (z == 2)

    barrier = pltpu.get_barrier_semaphore()
    for d in (d_core, d_x, d_y):
        pl.semaphore_signal(barrier, inc=1, device_id=d, device_id_type=MESH)
    @pl.when(z < 3)
    def _():
        pl.semaphore_signal(barrier, inc=1, device_id=right, device_id_type=MESH)
    @pl.when(z > 0)
    def _():
        pl.semaphore_signal(barrier, inc=1, device_id=left, device_id_type=MESH)
    pl.semaphore_wait(barrier, jnp.where(end, 4, 5))

    def cp(kind, k, src, dst, dev):
        return pltpu.make_async_remote_copy(src_ref=src, dst_ref=dst, send_sem=ssem.at[kind, k],
            recv_sem=rsem.at[kind, k], device_id=dev, device_id_type=MESH)

    def ctx(k):
        par = k % 2
        f = x * (1 - par) + y * par
        d_first = (dp + (1 - par) * (2 - 4 * x) + par * (4 - 8 * y), z)
        d_last = (dp + par * (2 - 4 * x) + (1 - par) * (4 - 8 * y), z)
        return f, d_first, d_last

    def rows(start, n):
        return pl.ds(pl.multiple_of(start, 16), n)
    def cols(start, n):
        return pl.ds(pl.multiple_of(start, 128), n)
    keep = rows(c * HR, HR)
    give = rows((1 - c) * HR, HR)

    def c_core(k):
        return cp(CORE, k, part.at[k % 2, give], r0.at[k], d_core)
    def c_first(k):
        f, d_first, _ = ctx(k)
        return cp(FIRST, k, r0.at[k, :, cols((1 - f) * HC, HC)], r1.at[k], d_first)
    def c_za(k):
        src = r1.at[k, rows(jnp.where(is0, SR, 0), 3 * SR)]
        return cp(ZA, k, src, za.at[k], (dp, jnp.where(is0, 1, 2)))
    def c_zb(k):
        src = r1.at[k, rows(jnp.where(is1, 2 * SR, 0), 2 * SR)]
        return cp(ZB, k, src, zb.at[k], (dp, jnp.where(is1, 2, 1)))
    def c_zc(k):
        src = r1.at[k, rows(jnp.where(is1, 0, 3 * SR), SR)]
        return cp(ZC, k, src, zc.at[k], (dp, jnp.where(is1, 0, 3)))
    def c_last(k):
        _, _, d_last = ctx(k)
        return cp(LAST, k, r1.at[k, rows(z * SR, SR)], ry.at[k], d_last)
    def place(k, shard, n=1):
        f, _, _ = ctx(k)
        return g_out.at[k, rows(c * HR + shard * SR, n * SR), cols(f * HC, HC)]
    def c_gr(k):
        return cp(GR, k, fin.at[k], place(k, z), right)
    def c_gl(k):
        return cp(GL, k, fin.at[k], place(k, z), left)
    def c_own(k):
        return pltpu.make_async_copy(fin.at[k], place(k, z), lsem.at[k])
    def c_gf(k):
        s = jnp.where(is1, 0, 3)
        return cp(GF, k, place(k, s), place(k, s), (dp, jnp.where(is1, 2, 1)))
    def c_ge(k):
        s = jnp.where(is1, 2, 0)
        return cp(GE, k, place(k, s, 2), place(k, s, 2), (dp, jnp.where(is1, 0, 3)))
    def c_agf(k):
        f, d_first, _ = ctx(k)
        blk = g_out.at[k, keep, cols(f * HC, HC)]
        return cp(AGF, k, blk, blk, d_first)
    def c_agc(k):
        blk = g_out.at[k, keep]
        return cp(AGC, k, blk, blk, d_core)

    def add(a, b):
        return (a.astype(jnp.float32) + b.astype(jnp.float32)).astype(jnp.bfloat16)

    def produce(k):
        def dot(l, lc, r, rc):
            return lax.dot_general(l[:, cols(lc * CR, CR)], r[:, cols(rc * CC, CC)], (((0,), (0,)), ((), ())),
                                   preferred_element_type=jnp.float32).astype(jnp.bfloat16)
        @pl.when(k < 8)
        def _():
            part[k % 2] = dot(act, k, d_ffn, 0)
        @pl.when((k >= 8) & (k < 16))
        def _():
            j = k - 8
            part[k % 2] = dot(low, j // 4, d_pre, j % 4)
        @pl.when((k >= 16) & (k < 18))
        def _():
            part[k % 2] = dot(att, k - 16, d_att, 0)
        @pl.when(k >= 18)
        def _():
            j = k - 18
            part[k % 2] = dot(tok, j // 3, d_proj, j % 3)

    def stage(s, k):
        if s == 0:
            @pl.when(k >= 2)
            def _(): c_core(k - 2).wait_send()
            produce(k)
            c_core(k).start()
        elif s == 1:
            c_core(k).wait_recv()
            r0[k] = add(r0[k], part[k % 2, keep])
            c_first(k).start()
        elif s == 2:
            f, _, _ = ctx(k)
            c_first(k).wait_recv()
            r1[k] = add(r1[k], r0[k, :, cols(f * HC, HC)])
            @pl.when(end)
            def _(): c_za(k).start()
        elif s == 3:
            @pl.when(mid)
            def _():
                c_za(k).wait_recv()
                own = rows(jnp.where(is1, SR, 0), 3 * SR)
                r1[k, own] = add(r1[k, own], za[k])
                c_zb(k).start()
        elif s == 4:
            @pl.when(mid)
            def _():
                c_zb(k).wait_recv()
                own = rows(jnp.where(is1, 0, 2 * SR), 2 * SR)
                r1[k, own] = add(r1[k, own], zb[k])
                c_zc(k).start()
        elif s == 5:
            @pl.when(end)
            def _():
                c_zc(k).wait_recv()
                own = rows(z * SR, SR)
                r1[k, own] = add(r1[k, own], zc[k])
            c_last(k).start()
        elif s == 6:
            c_last(k).wait_recv()
            fin[k] = add(r1[k, rows(z * SR, SR)], ry[k])
            c_own(k).start()
            @pl.when(z < 3)
            def _(): c_gr(k).start()
            @pl.when(z > 0)
            def _(): c_gl(k).start()
        elif s == 7:
            @pl.when(is1)
            def _(): c_gr(k).wait_recv()
            @pl.when(is2)
            def _(): c_gl(k).wait_recv()
            @pl.when(mid)
            def _(): c_gf(k).start()
        elif s == 8:
            @pl.when(is1)
            def _(): c_gl(k).wait_recv()
            @pl.when(is2)
            def _(): c_gr(k).wait_recv()
            @pl.when(mid)
            def _():
                c_gf(k).wait_recv()
                c_ge(k).start()
        elif s == 9:
            @pl.when(is0)
            def _(): c_gl(k).wait_recv()
            @pl.when(is3)
            def _(): c_gr(k).wait_recv()
            @pl.when(end)
            def _(): c_ge(k).wait_recv()
            c_own(k).wait()
            c_agf(k).start()
        elif s == 10:
            c_agf(k).wait_recv()
            c_agc(k).start()
        elif s == 11:
            c_agc(k).wait_recv()
            c_first(k).wait_send()
            c_last(k).wait_send()
            @pl.when(end)
            def _(): c_za(k).wait_send()
            @pl.when(mid)
            def _():
                c_zb(k).wait_send()
                c_zc(k).wait_send()
                c_gf(k).wait_send()
                c_ge(k).wait_send()
            @pl.when(z < 3)
            def _(): c_gr(k).wait_send()
            @pl.when(z > 0)
            def _(): c_gl(k).wait_send()
            c_agf(k).wait_send()
            c_agc(k).wait_send()

    def s_copy(i):
        dev = (d_core, d_x, d_y, (dp, jnp.where(is0, 1, 2)), (dp, jnp.where(is1, 2, 1)), (dp, jnp.where(is1, 0, 3)))[i]
        return pltpu.make_async_remote_copy(src_ref=sm.at[i], dst_ref=smr.at[i], send_sem=smss.at[i], recv_sem=smrs.at[i],
            device_id=dev, device_id_type=MESH)
    sm[0] = small[...]
    def s_step(i):
        if i > 0:
            sends = (None, None, None, end, mid, mid)[i - 1]
            gets = (None, None, None, mid, mid, end)[i - 1]
            def get():
                s_copy(i - 1).wait_recv()
                if i == 6:
                    sm[i] = smr[i - 1]
                else:
                    sm[i] = sm[i - 1] + smr[i - 1]
            if gets is None:
                get()
            else:
                pl.when(gets)(get)
                @pl.when(jnp.logical_not(gets))
                def _(): sm[i] = sm[i - 1]
        if i < 6:
            sends = (None, None, None, end, mid, mid)[i]
            if sends is None:
                s_copy(i).start()
            else:
                pl.when(sends)(lambda: s_copy(i).start())

    def tick(t, _):
        for s in range(len(OFF) - 1, -1, -1):
            k = t - OFF[s]
            @pl.when((k >= 0) & (k < N))
            def _():
                stage(s, k)
        for i in range(7):
            @pl.when(t == N + i)
            def _():
                s_step(i)
        return 0
    lax.fori_loop(0, N + OFF[-1], tick, 0)
    for i in range(6):
        sends = (None, None, None, end, mid, mid)[i]
        if sends is None:
            s_copy(i).wait_send()
        else:
            pl.when(sends)(lambda: s_copy(i).wait_send())
    @pl.when(mid)
    def _(): small_out[...] = sm[5]
    @pl.when(end)
    def _(): small_out[...] = sm[6]
    for k in (N - 2, N - 1):
        c_core(k).wait_send()

def sum_grads(act, d_ffn, low, d_pre, att, d_att, tok, d_proj, small):
    B = jnp.bfloat16
    V = pl.BlockSpec(memory_space=pltpu.VMEM)
    return pl.pallas_call(grads_kernel,
        out_shape=[jax.ShapeDtypeStruct((N, CR, CC), B), jax.ShapeDtypeStruct(small.shape, jnp.float32)],
        in_specs=[V] * 9,
        out_specs=[pl.BlockSpec(memory_space=pltpu.HBM), V],
        scratch_shapes=[
            pltpu.VMEM((2, CR, CC), B), pltpu.VMEM((N, HR, CC), B), pltpu.VMEM((N, HR, HC), B),
            pltpu.VMEM((N, 3 * SR, HC), B), pltpu.VMEM((N, 2 * SR, HC), B), pltpu.VMEM((N, SR, HC), B),
            pltpu.VMEM((N, SR, HC), B), pltpu.VMEM((N, SR, HC), B),
            pltpu.VMEM((7,) + small.shape, jnp.float32), pltpu.VMEM((6,) + small.shape, jnp.float32),
            pltpu.SemaphoreType.DMA((KINDS, N)), pltpu.SemaphoreType.DMA((KINDS, N)), pltpu.SemaphoreType.DMA((N,)),
            pltpu.SemaphoreType.DMA((6,)), pltpu.SemaphoreType.DMA((6,)),
        ],
        compiler_params=pltpu.CompilerParams(collective_id=0, has_side_effects=True, vmem_limit_bytes=60 * 2**20),
        name="grads",
    )(act, d_ffn, low, d_pre, att, d_att, tok, d_proj, small)


def widen_kernel(g, contract, expand, mixing, projection):
    i = pl.program_id(0)
    for ref, first, last in ((contract, 0, 8), (expand, 8, 16), (mixing, 16, 18), (projection, 18, 24)):
        @pl.when((i >= first) & (i < last))
        def _():
            ref[...] = g[0].astype(F32)


def widen(g):
    def spec(first, count, across):
        def place(i):
            j = jnp.clip(i - first, 0, count - 1)
            return (j // across, j % across)
        return pl.BlockSpec((CR, CC), place)
    shape = lambda r, c: jax.ShapeDtypeStruct((r, c), F32)
    return pl.pallas_call(widen_kernel, grid=(N,),
        in_specs=[pl.BlockSpec((1, CR, CC), lambda i: (i, 0, 0))],
        out_specs=[spec(0, 8, 1), spec(8, 8, 4), spec(16, 2, 1), spec(18, 6, 3)],
        out_shape=[shape(4 * D, D), shape(D, 4 * D), shape(D, D), shape(D, 3 * D)],
        compiler_params=pltpu.CompilerParams(vmem_limit_bytes=40 * 2**20),
        cost_estimate=pl.CostEstimate(flops=0, bytes_accessed=6 * N * CR * CC, transcendentals=0),
        name="widen")(g)


def deal(blocks):
    z = lax.axis_index("blk")
    n = blocks.shape[0]
    out = jnp.zeros_like(blocks)
    for m in range(n):
        piece = lax.dynamic_index_in_dim(blocks, z ^ m, 0)
        if m:
            piece = lax.ppermute(piece, "blk", [(i, i ^ m) for i in range(n)])
        out = lax.dynamic_update_slice(out, piece, (z ^ m,) + (0,) * (blocks.ndim - 1))
    return out


def layer_norm(hidden, gain_vec, shift_vec):
    row_mean = jnp.mean(hidden, axis=-1, keepdims=True)
    centered = hidden - row_mean
    variance = jnp.mean(centered * centered, axis=-1, keepdims=True)
    return centered * lax.rsqrt(variance + norm_eps) * gain_vec + shift_vec


def local(tokens, row_kinds, live_mask, keep_flag, projection, proj_bias, mixing, mix_bias, attn_gain, attn_shift,
          expand, expand_bias, contract, contract_bias, ffn_gain, ffn_shift, cotangent):
    row_count, block_len, _ = tokens.shape
    blocks = lax.axis_size("blk")
    length = block_len * blocks
    z = lax.axis_index("blk")
    f32 = lambda a: a.astype(F32)
    row = deal(tokens).reshape(length, D)
    live = deal(live_mask[:, None]).reshape(length)
    cot = deal(cotangent).reshape(length, D)
    kind = lax.dynamic_index_in_dim(row_kinds, z, 0, False)
    keep = lax.dynamic_index_in_dim(keep_flag, z, 0, False) > 0

    seg = jnp.arange(length, dtype=jnp.int32) // jnp.where(kind == 0, DOC_SHORT, length)
    allowed = (seg[:, None] == seg[None, :]) & (live[None, :] > 0)
    bias = jnp.where(allowed, 0.0, NEG).astype(F32)
    qkv_bias = jnp.concatenate([f32(proj_bias[0]), jnp.zeros((D,), F32), f32(proj_bias[1])])
    qkv = (dot(row, projection) + qkv_bias).astype(B16)
    attended, probs = attend(qkv, bias)

    attn_out = dot(attended, mixing) + f32(mix_bias)
    normed, norm_one_back = jax.vjp(layer_norm, f32(row) + attn_out, f32(attn_gain), f32(attn_shift))
    normed_low = normed.astype(B16)
    pre_act = dot(normed_low, expand) + f32(expand_bias)
    gelu_value, gelu_back = jax.vjp(functools.partial(jax.nn.gelu, approximate=False), pre_act)
    activated = gelu_value.astype(B16)
    ffn_out = dot(activated, contract) + f32(contract_bias)
    normed_two, norm_two_back = jax.vjp(layer_norm, normed + ffn_out, f32(ffn_gain), f32(ffn_shift))
    layer_out = jnp.where(keep, normed_two, f32(row)).astype(B16)
    layer_out = deal(layer_out.reshape(blocks, block_len, D))

    grad_two = jnp.where(keep, f32(cot), 0.0)
    d_resid_two, ffn_gain_grad, ffn_shift_grad = norm_two_back(grad_two)
    d_ffn = d_resid_two.astype(B16)
    d_act = dot(d_ffn, contract, NT)
    d_pre = gelu_back(d_act)[0].astype(B16)
    d_normed = d_resid_two + dot(d_pre, expand, NT)
    d_resid_one, attn_gain_grad, attn_shift_grad = norm_one_back(d_normed)
    d_attn = d_resid_one.astype(B16)
    d_attended = dot(d_attn, mixing, NT).astype(B16)
    d_proj = jnp.concatenate(attend_back(qkv, probs, d_attended), axis=1)
    d_tokens = d_resid_one + dot(d_proj, projection, NT)
    tokens_grad = jnp.where(keep, d_tokens, f32(cot)).astype(B16)
    tokens_grad = deal(tokens_grad.reshape(blocks, block_len, D)).astype(F32)

    total = lambda a: jnp.sum(f32(a), axis=0)
    small = jnp.concatenate([total(d_proj[:, :D]), total(d_proj[:, 2 * D:]), total(d_attn), attn_gain_grad, attn_shift_grad,
        total(d_pre), total(d_ffn), ffn_gain_grad, ffn_shift_grad, jnp.zeros((4 * D,), F32)]).reshape(16, D)
    g, small = sum_grads(activated, d_ffn, normed_low, d_pre, attended, d_attn, row, d_proj, small)
    groups = lax.axis_size("dp") // 8
    if groups > 1:
        index = [[i + 8 * j for j in range(groups)] for i in range(8)]
        g, small = lax.psum((g, small), "dp", axis_index_groups=index)
    contract_grad, expand_grad, mixing_grad, projection_grad = widen(g)
    return (layer_out, tokens_grad, projection_grad, small[:2], mixing_grad, small[2], small[3], small[4], expand_grad,
            small[5:9].reshape(-1), contract_grad, small[9], small[10], small[11])


def solution(mesh):
    data = P("dp", "blk", None)
    in_specs = (data, P("dp"), P("dp", "blk"), P("dp")) + (P(),) * 12 + (data,)
    out_specs = (data, data) + (P(),) * 12
    return jax.shard_map(local, mesh=mesh, in_specs=in_specs, out_specs=out_specs, check_vma=False)
```

```python
import functools

import jax
import jax.numpy as jnp
from jax import lax
from jax.experimental import pallas as pl
from jax.experimental.pallas import tpu as pltpu
from jax.sharding import PartitionSpec as P

D = 768
FF = 3072
HEADS = 12
HEAD_DIM = 64
DOC_SHORT = 128
MESH = pl.DeviceIdType.MESH
EPS = 1e-05
NEG = -1e9
F32, B16 = jnp.float32, jnp.bfloat16
NN = (((1,), (0,)), ((), ()))
NT = (((1,), (1,)), ((), ()))
TN = (((0,), (0,)), ((), ()))

CR, CC = 384, 768
HR, HC = CR // 2, CC // 2
SR = HR // 4
N = 24
KINDS = 12
CORE, FIRST, ZA, ZB, ZC, LAST, GR, GL, GF, GE, AGF, AGC = range(KINDS)
OFF = [0, 1, 4, 6, 8, 10, 12, 14, 16, 18, 21, 22]
VECS = 16


def dot(a, b, dims=NN):
    return lax.dot_general(a, b, dims, preferred_element_type=F32)


def rows(start, n):
    return pl.ds(pl.multiple_of(start, 16), n)


def cols(start, n):
    return pl.ds(pl.multiple_of(start, 128), n)


def normal_parts(v):
    t = 1.0 / (1.0 + (0.3275911 * 0.5 ** 0.5) * jnp.abs(v))
    ex = jnp.exp(-0.5 * (v * v))
    poly = t * (0.127414796 + t * (-0.142248368 + t * (0.7107068705 + t * (-0.7265760135 + t * 0.5307027145))))
    tail = poly * ex
    below = jnp.where(v < 0, tail, 1.0 - tail)
    return v * below, below + v * (ex * 0.3989422804014327)


def mean(a):
    return jnp.sum(a, axis=1, keepdims=True) * (1.0 / D)


def layer_kernel(kinds, keeps, vecs, ebias, live, tokens, cot_in, w_proj, w_mix, w_exp, w_con,
                 g_out, small_out, out_l, out_t,
                 wproj, wmix, wexp, wcon, row, cot, livebuf, qkv, att, probs, low, act, gp, xhat, dres, d_ffn, d_attn, d_att,
                 send, rstd, bias,
                 part, r0, r1, za, zb, zc, fin, sm, smr,
                 ssem, rsem, lsem, smss, smrs, wsem, dsend, drecv, dloc):
    dp, z = lax.axis_index("dp"), lax.axis_index("blk")
    T = row.shape[0]
    BL = T // 4
    c, x, y = dp % 2, (dp // 2) % 2, (dp // 4) % 2
    d_core = (dp + 1 - 2 * c, z)
    d_x = (dp + 2 - 4 * x, z)
    d_y = (dp + 4 - 8 * y, z)
    right, left = (dp, jnp.minimum(z + 1, 3)), (dp, jnp.maximum(z - 1, 0))
    is0, is1, is2, is3 = z == 0, z == 1, z == 2, z == 3
    end, mid = (z == 0) | (z == 3), (z == 1) | (z == 2)
    others = (z, z + 1 - 2 * (z % 2), z + 2 - 4 * (z // 2), 3 - z)

    loads = [pltpu.make_async_copy(a, b, wsem.at[i]) for i, (a, b) in
             enumerate(((w_proj, wproj), (w_mix, wmix), (w_exp, wexp), (w_con, wcon)))]

    barrier = pltpu.get_barrier_semaphore()
    for d in (d_core, d_x, d_y) + tuple((dp, others[m]) for m in (1, 2, 3)):
        pl.semaphore_signal(barrier, inc=1, device_id=d, device_id_type=MESH)
    pl.semaphore_wait(barrier, 6)

    TOK, LIVE, COT, OUTL, OUTT = range(5)

    def deal(kind, m, arriving=False):
        there = others[m]
        src, dst = {
            TOK: lambda: (tokens.at[there], row.at[rows((there if arriving else z) * BL, BL)]),
            LIVE: lambda: (live.at[there], livebuf.at[there if arriving else z]),
            COT: lambda: (cot_in.at[there], cot.at[rows((there if arriving else z) * BL, BL)]),
            OUTL: lambda: (send.at[rows(there * BL, BL)], out_l.at[there if arriving else z]),
            OUTT: lambda: (send.at[rows(there * BL, BL)], out_t.at[there if arriving else z]),
        }[kind]()
        if m == 0:
            return pltpu.make_async_copy(src, dst, dloc.at[kind])
        return pltpu.make_async_remote_copy(src_ref=src, dst_ref=dst, send_sem=dsend.at[kind, m], recv_sem=drecv.at[kind, m],
                                            device_id=(dp, there), device_id_type=MESH)

    def finish(kind):
        for m in (1, 2, 3):
            deal(kind, m).wait_send()

    for m in (3, 2, 1, 0):
        deal(LIVE, m).start()
        deal(TOK, m).start()
    for load in loads:
        load.start()

    def project(m):
        (deal(TOK, 0).wait if m == 0 else deal(TOK, m, True).wait_recv)()
        r = rows(others[m] * BL, BL)
        for j in range(3):
            s = slice(j * D, (j + 1) * D)
            part_j = dot(row[r], wproj[:, s]) + vecs[j:j + 1]
            if j == 0:
                part_j = part_j.astype(B16).astype(F32) * HEAD_DIM ** -0.5
            qkv[r, s] = part_j.astype(B16)

    loads[0].wait()
    for m in (0, 1, 2, 3):
        project(m)
    for m in (3, 2, 1, 0):
        deal(COT, m).start()

    deal(LIVE, 0).wait()
    for m in (1, 2, 3):
        deal(LIVE, m, True).wait_recv()
    count = jnp.sum(jnp.sum(livebuf[...], axis=0), axis=1, keepdims=True)
    short = (1 - kinds[z]).astype(F32) * NEG
    for b in range(4):
        key = lax.broadcasted_iota(jnp.int32, (BL, T), 0) + b * BL
        query = lax.broadcasted_iota(jnp.int32, (BL, T), 1)
        shift = DOC_SHORT.bit_length() - 1
        apart = jnp.where((key >> shift) == (query >> shift), 0.0, short)
        bias[b * BL:(b + 1) * BL] = jnp.where(key < count, apart, NEG)

    def attend(i, _):
        s = cols(i * 2 * HEAD_DIM, 2 * HEAD_DIM)
        q2, k2, v2 = (qkv[:, cols(j * D + i * 2 * HEAD_DIM, 2 * HEAD_DIM)] for j in range(3))
        outs = []
        for h in range(2):
            hs = slice(h * HEAD_DIM, (h + 1) * HEAD_DIM)
            scores = dot(k2[:, hs], q2[:, hs], NT) + bias[...]
            e = jnp.exp(scores - jnp.max(scores, axis=0, keepdims=True))
            p = (e * (1.0 / jnp.sum(e, axis=0, keepdims=True))).astype(B16)
            probs[2 * i + h] = p
            outs.append(dot(v2[:, hs], p, TN))
        att[:, s] = jnp.concatenate(outs, axis=0).T.astype(B16)
        return 0
    lax.fori_loop(0, HEADS // 2, attend, 0)

    loads[1].wait()
    RB = 256

    def norm_one(i, _):
        r = rows(i * RB, RB)
        h = row[r].astype(F32) + (dot(att[r], wmix[...]) + vecs[3:4])
        h = h - mean(h)
        rs = lax.rsqrt(mean(h * h) + EPS)
        h = h * rs
        xhat[r] = h
        rstd[r] = rs
        low[r] = (h * vecs[4:5] + vecs[5:6]).astype(B16)
        return 0
    lax.fori_loop(0, T // RB, norm_one, 0)

    loads[2].wait()
    loads[3].wait()
    dres[...] = jnp.zeros_like(dres)

    def feed(j, _):
        s = cols(j * CR, CR)
        pre = dot(low[...], wexp[:, s]) + ebias[j]
        value, slope = normal_parts(pre)
        value = value.astype(B16)
        act[:, s] = value
        gp[:, s] = slope.astype(B16)
        dres[...] += dot(value, wcon[rows(j * CR, CR)])
        return 0
    lax.fori_loop(0, FF // CR, feed, 0)

    keep = keeps[z].astype(F32)
    for kind in (COT,):
        deal(kind, 0).wait()
        for m in (1, 2, 3):
            deal(kind, m, True).wait_recv()
    sm[0] = jnp.zeros((VECS, D), F32)

    def norm_two(i, _):
        r = rows(i * BL, BL)
        h = (xhat[r] * vecs[4:5] + vecs[5:6]) + (dres[r] + vecs[6:7])
        h = h - mean(h)
        rs = lax.rsqrt(mean(h * h) + EPS)
        h = h * rs
        send[r] = jnp.where(keep > 0, h * vecs[7:8] + vecs[8:9], row[r].astype(F32)).astype(B16)
        grad = cot[r].astype(F32) * keep
        sm[0, 10:11] += jnp.sum(grad * h, axis=0, keepdims=True)
        sm[0, 11:12] += jnp.sum(grad, axis=0, keepdims=True)
        dx = grad * vecs[7:8]
        dr = rs * (dx - mean(dx) - h * mean(dx * h))
        dres[r] = dr
        dr = dr.astype(B16)
        d_ffn[r] = dr
        sm[0, 9:10] += jnp.sum(dr.astype(F32), axis=0, keepdims=True)
        return 0
    lax.fori_loop(0, T // BL, norm_two, 0)
    for m in (3, 2, 1, 0):
        deal(OUTL, m).start()

    def back_feed(j):
        s = cols(j * CR, CR)
        d_pre = (dot(d_ffn[...], wcon[rows(j * CR, CR)], NT) * gp[:, s].astype(F32)).astype(B16)
        gp[:, s] = d_pre
        dres[...] += dot(d_pre, wexp[:, s], NT)

    def back_norm():
        for q in range(FF // D):
            sm[0, 5 + q:6 + q] = jnp.sum(gp[:, q * D:(q + 1) * D].astype(F32), axis=0, keepdims=True)

        def block(i, _):
            r = rows(i * BL, BL)
            dn, h = dres[r], xhat[r]
            sm[0, 3:4] += jnp.sum(dn * h, axis=0, keepdims=True)
            sm[0, 4:5] += jnp.sum(dn, axis=0, keepdims=True)
            dx = dn * vecs[4:5]
            dr = rstd[r] * (dx - mean(dx) - h * mean(dx * h))
            dres[r] = dr
            dr = dr.astype(B16)
            d_attn[r] = dr
            sm[0, 2:3] += jnp.sum(dr.astype(F32), axis=0, keepdims=True)
            return 0
        lax.fori_loop(0, T // BL, block, 0)
        d_att[...] = dot(d_attn[...], wmix[...], NT).astype(B16)

    def back_attend(i):
        q2, k2, v2 = (qkv[:, cols(j * D + i * 2 * HEAD_DIM, 2 * HEAD_DIM)] for j in range(3))
        da2 = d_att[:, cols(i * 2 * HEAD_DIM, 2 * HEAD_DIM)]
        dqs, dks, dvs = [], [], []
        for h in range(2):
            hs = slice(h * HEAD_DIM, (h + 1) * HEAD_DIM)
            p = probs[2 * i + h]
            dp_t = dot(v2[:, hs], da2[:, hs], NT)
            pf = p.astype(F32)
            delta = jnp.sum(pf * dp_t, axis=0, keepdims=True)
            ds = (pf * (dp_t - delta)).astype(B16)
            dqs.append(dot(k2[:, hs], ds, TN))
            dks.append(dot(ds, q2[:, hs]))
            dvs.append(dot(p, da2[:, hs]))
        dq = (jnp.concatenate(dqs, axis=0) * HEAD_DIM ** -0.5).T
        dk, dv = jnp.concatenate(dks, axis=1), jnp.concatenate(dvs, axis=1)
        for j, d in enumerate((dq, dk, dv)):
            qkv[:, cols(j * D + i * 2 * HEAD_DIM, 2 * HEAD_DIM)] = d.astype(B16)

    def back_sums():
        sm[0, 0:1] = jnp.sum(qkv[:, 0:D].astype(F32), axis=0, keepdims=True)
        sm[0, 1:2] = jnp.sum(qkv[:, 2 * D:].astype(F32), axis=0, keepdims=True)

    def back_tokens(m):
        if m == 0:
            deal(OUTL, 0).wait()
            finish(OUTL)
        r = rows(others[m] * BL, BL)
        d = dres[r] + dot(qkv[r], wproj[...], NT)
        send[r] = jnp.where(keep > 0, d, cot[r].astype(F32)).astype(B16)
        deal(OUTT, m).start()

    def cp(kind, k, src, dst, dev):
        return pltpu.make_async_remote_copy(src_ref=src, dst_ref=dst, send_sem=ssem.at[kind, k],
                                            recv_sem=rsem.at[kind, k], device_id=dev, device_id_type=MESH)

    def way(k):
        par = k % 2
        f = x * (1 - par) + y * par
        d_first = (dp + (1 - par) * (2 - 4 * x) + par * (4 - 8 * y), z)
        d_last = (dp + par * (2 - 4 * x) + (1 - par) * (4 - 8 * y), z)
        return f, d_first, d_last

    keep_rows = rows(c * HR, HR)
    give_rows = rows((1 - c) * HR, HR)

    def c_core(k):
        return cp(CORE, k, part.at[k % 2, give_rows], r0.at[k], d_core)

    def c_first(k):
        f, d_first, _ = way(k)
        return cp(FIRST, k, r0.at[k, :, cols((1 - f) * HC, HC)], r1.at[k], d_first)

    def c_za(k):
        return cp(ZA, k, r1.at[k, rows(jnp.where(is0, SR, 0), 3 * SR)], za.at[k], (dp, jnp.where(is0, 1, 2)))

    def c_zb(k):
        return cp(ZB, k, r1.at[k, rows(jnp.where(is1, 2 * SR, 0), 2 * SR)], zb.at[k], (dp, jnp.where(is1, 2, 1)))

    def c_zc(k):
        return cp(ZC, k, r1.at[k, rows(jnp.where(is1, 0, 3 * SR), SR)], zc.at[k], (dp, jnp.where(is1, 0, 3)))

    def c_last(k):
        _, _, d_last = way(k)
        return cp(LAST, k, r1.at[k, rows(z * SR, SR)], fin.at[k], d_last)

    def place(k, shard, n=1):
        f, _, _ = way(k)
        return g_out.at[k, rows(c * HR + shard * SR, n * SR), cols(f * HC, HC)]

    def c_gr(k):
        return cp(GR, k, fin.at[k], place(k, z), right)

    def c_gl(k):
        return cp(GL, k, fin.at[k], place(k, z), left)

    def c_own(k):
        return pltpu.make_async_copy(fin.at[k], place(k, z), lsem.at[k])

    def c_gf(k):
        s = jnp.where(is1, 0, 3)
        return cp(GF, k, place(k, s), place(k, s), (dp, jnp.where(is1, 2, 1)))

    def c_ge(k):
        s = jnp.where(is1, 2, 0)
        return cp(GE, k, place(k, s, 2), place(k, s, 2), (dp, jnp.where(is1, 0, 3)))

    def c_agf(k):
        f, d_first, _ = way(k)
        block = g_out.at[k, keep_rows, cols(f * HC, HC)]
        return cp(AGF, k, block, block, d_first)

    def c_agc(k):
        block = g_out.at[k, keep_rows]
        return cp(AGC, k, block, block, d_core)

    def add(a, b):
        return (a.astype(F32) + b.astype(F32)).astype(B16)

    def produce(k):
        def piece(l, lc, r, rc):
            part[k % 2] = dot(l[:, cols(lc * CR, CR)], r[:, cols(rc * CC, CC)], TN).astype(B16)

        @pl.when(k < 8)
        def _():
            piece(act, k, d_ffn, 0)

        @pl.when((k >= 8) & (k < 16))
        def _():
            piece(low, (k - 8) // 4, gp, (k - 8) % 4)

        @pl.when((k >= 16) & (k < 18))
        def _():
            piece(att, k - 16, d_attn, 0)

        @pl.when(k >= 18)
        def _():
            piece(row, (k - 18) // 3, qkv, (k - 18) % 3)

    def stage(s, k):
        if s == 0:
            @pl.when(k >= 2)
            def _():
                c_core(k - 2).wait_send()
            produce(k)
            c_core(k).start()
        elif s == 1:
            c_core(k).wait_recv()
            r0[k] = add(r0[k], part[k % 2, keep_rows])
            c_first(k).start()
        elif s == 2:
            f, _, _ = way(k)
            c_first(k).wait_recv()
            r1[k] = add(r1[k], r0[k, :, cols(f * HC, HC)])

            @pl.when(end)
            def _():
                c_za(k).start()
        elif s == 3:
            @pl.when(mid)
            def _():
                c_za(k).wait_recv()
                own = rows(jnp.where(is1, SR, 0), 3 * SR)
                r1[k, own] = add(r1[k, own], za[k])
                c_zb(k).start()
        elif s == 4:
            @pl.when(mid)
            def _():
                c_zb(k).wait_recv()
                own = rows(jnp.where(is1, 0, 2 * SR), 2 * SR)
                r1[k, own] = add(r1[k, own], zb[k])
                c_zc(k).start()
        elif s == 5:
            @pl.when(end)
            def _():
                c_zc(k).wait_recv()
                own = rows(z * SR, SR)
                r1[k, own] = add(r1[k, own], zc[k])
            c_last(k).start()
        elif s == 6:
            c_last(k).wait_recv()
            fin[k] = add(r1[k, rows(z * SR, SR)], fin[k])
            c_own(k).start()

            @pl.when(z < 3)
            def _():
                c_gr(k).start()

            @pl.when(z > 0)
            def _():
                c_gl(k).start()
        elif s == 7:
            @pl.when(is1)
            def _():
                c_gr(k).wait_recv()

            @pl.when(is2)
            def _():
                c_gl(k).wait_recv()

            @pl.when(mid)
            def _():
                c_gf(k).start()
        elif s == 8:
            @pl.when(is1)
            def _():
                c_gl(k).wait_recv()

            @pl.when(is2)
            def _():
                c_gr(k).wait_recv()

            @pl.when(mid)
            def _():
                c_gf(k).wait_recv()
                c_ge(k).start()
        elif s == 9:
            @pl.when(is0)
            def _():
                c_gl(k).wait_recv()

            @pl.when(is3)
            def _():
                c_gr(k).wait_recv()

            @pl.when(end)
            def _():
                c_ge(k).wait_recv()
            c_own(k).wait()
            c_agf(k).start()
        elif s == 10:
            c_agf(k).wait_recv()
            c_agc(k).start()
        elif s == 11:
            c_agc(k).wait_recv()
            c_first(k).wait_send()
            c_last(k).wait_send()

            @pl.when(end)
            def _():
                c_za(k).wait_send()

            @pl.when(mid)
            def _():
                c_zb(k).wait_send()
                c_zc(k).wait_send()
                c_gf(k).wait_send()
                c_ge(k).wait_send()

            @pl.when(z < 3)
            def _():
                c_gr(k).wait_send()

            @pl.when(z > 0)
            def _():
                c_gl(k).wait_send()
            c_agf(k).wait_send()
            c_agc(k).wait_send()

    steps = ((d_core, None, None), (d_x, None, None), (d_y, None, None),
             ((dp, jnp.where(is0, 1, 2)), end, mid), ((dp, jnp.where(is1, 2, 1)), mid, mid), ((dp, jnp.where(is1, 0, 3)), mid, end))

    def only(cond, f):
        f() if cond is None else pl.when(cond)(f)

    def s_copy(i):
        return pltpu.make_async_remote_copy(src_ref=sm.at[i], dst_ref=smr.at[i], send_sem=smss.at[i], recv_sem=smrs.at[i],
                                            device_id=steps[i][0], device_id_type=MESH)

    def small_step(i):
        if i > 0:
            sm[i] = sm[i - 1]

            def get():
                s_copy(i - 1).wait_recv()
                sm[i] = smr[i - 1] if i == 6 else sm[i - 1] + smr[i - 1]
            only(steps[i - 1][2], get)
        if i < 6:
            only(steps[i][1], lambda: s_copy(i).start())

    def tick(t, _):
        for s in range(len(OFF) - 1, -1, -1):
            k = t - OFF[s]

            @pl.when((k >= 0) & (k < N))
            def _():
                stage(s, k)

        @pl.when(t < 8)
        def _():
            back_feed(t)

        @pl.when(t == 8)
        def _():
            back_norm()

        @pl.when((t >= 9) & (t < 15))
        def _():
            back_attend(t - 9)

        @pl.when(t == 15)
        def _():
            back_sums()
        for m in range(4):
            @pl.when(t == 16 + m)
            def _():
                back_tokens(m)
        for i in range(7):
            @pl.when(t == N + i)
            def _():
                small_step(i)
        return 0
    lax.fori_loop(0, N + OFF[-1], tick, 0)

    small_out[...] = sm[6]
    for i in range(6):
        only(steps[i][1], lambda: s_copy(i).wait_send())
    for k in (N - 2, N - 1):
        c_core(k).wait_send()
    deal(OUTT, 0).wait()
    for kind in (TOK, LIVE, COT, OUTT):
        finish(kind)
    for m in (1, 2, 3):
        deal(OUTL, m, True).wait_recv()
        deal(OUTT, m, True).wait_recv()


def run_layer(kinds, keeps, vecs, ebias, live, tokens, cot, *weights):
    blocks, BL, _ = tokens.shape
    T = blocks * BL
    V, S, H = (pl.BlockSpec(memory_space=m) for m in (pltpu.VMEM, pltpu.SMEM, pltpu.HBM))
    low16 = lambda *s: pltpu.VMEM(s, B16)
    full = lambda *s: pltpu.VMEM(s, F32)
    sem = lambda *s: pltpu.SemaphoreType.DMA(s)
    return pl.pallas_call(
        layer_kernel,
        out_shape=[jax.ShapeDtypeStruct((N, CR, CC), B16), jax.ShapeDtypeStruct((VECS, D), F32),
                   jax.ShapeDtypeStruct(tokens.shape, B16), jax.ShapeDtypeStruct(tokens.shape, B16)],
        in_specs=[S, S, V, V, V, H, H, H, H, H, H],
        out_specs=[H, V, H, H],
        scratch_shapes=[
            low16(D, 3 * D), low16(D, D), low16(D, FF), low16(FF, D),
            low16(T, D), low16(T, D), pltpu.VMEM((blocks, 1, BL), jnp.int32), low16(T, 3 * D), low16(T, D), low16(HEADS, T, T),
            low16(T, D), low16(T, FF), low16(T, FF), full(T, D), full(T, D), low16(T, D), low16(T, D), low16(T, D),
            low16(T, D), full(T, 1), full(T, T),
            low16(2, CR, CC), low16(N, HR, CC), low16(N, HR, HC), low16(N, 3 * SR, HC), low16(N, 2 * SR, HC), low16(N, SR, HC),
            low16(N, SR, HC), full(7, VECS, D), full(6, VECS, D),
            sem(KINDS, N), sem(KINDS, N), sem(N), sem(6), sem(6), sem(4), sem(5, 4), sem(5, 4), sem(5),
        ],
        compiler_params=pltpu.CompilerParams(collective_id=0, has_side_effects=True, vmem_limit_bytes=63 * 2**20),
        name="layer",
    )(kinds, keeps, vecs, ebias, live, tokens, cot, *weights)


def widen_kernel(g, contract, expand, mixing, projection):
    i = pl.program_id(0)
    for ref, first, last in ((contract, 0, 8), (expand, 8, 16), (mixing, 16, 18), (projection, 18, 24)):
        @pl.when((i >= first) & (i < last))
        def _():
            ref[...] = g[0].astype(F32)


def widen(g):
    def spec(first, count, across):
        def place(i):
            j = jnp.clip(i - first, 0, count - 1)
            return (j // across, j % across)
        return pl.BlockSpec((CR, CC), place)
    shape = lambda r, c: jax.ShapeDtypeStruct((r, c), F32)
    return pl.pallas_call(
        widen_kernel, grid=(N,),
        in_specs=[pl.BlockSpec((1, CR, CC), lambda i: (i, 0, 0))],
        out_specs=[spec(0, 8, 1), spec(8, 8, 4), spec(16, 2, 1), spec(18, 6, 3)],
        out_shape=[shape(FF, D), shape(D, FF), shape(D, D), shape(D, 3 * D)],
        compiler_params=pltpu.CompilerParams(vmem_limit_bytes=40 * 2**20),
        cost_estimate=pl.CostEstimate(flops=0, bytes_accessed=6 * N * CR * CC, transcendentals=0),
        name="widen",
    )(g)


def local(tokens, row_kinds, live_mask, keep_flag, projection, proj_bias, mixing, mix_bias, attn_gain, attn_shift,
          expand, expand_bias, contract, contract_bias, ffn_gain, ffn_shift, cotangent):
    f32 = lambda a: a.astype(F32)
    pieces = [(0, proj_bias[0]), (2, proj_bias[1]), (3, mix_bias), (4, attn_gain), (5, attn_shift), (6, contract_bias),
              (7, ffn_gain), (8, ffn_shift)]
    vecs = sum(jnp.pad(f32(v)[None], ((i, VECS - 1 - i), (0, 0))) for i, v in pieces)
    ebias = f32(expand_bias).reshape(FF // CR, 1, CR)
    g, small, layer_out, tokens_grad = run_layer(row_kinds, keep_flag, vecs, ebias, live_mask[:, None], tokens, cotangent,
                                                 projection, mixing, expand, contract)
    groups = lax.axis_size("dp") // 8
    if groups > 1:
        index = [[i + 8 * j for j in range(groups)] for i in range(8)]
        g, small = lax.psum((g, small), "dp", axis_index_groups=index)
    contract_grad, expand_grad, mixing_grad, projection_grad = widen(g)
    return (layer_out, f32(tokens_grad), projection_grad, small[:2], mixing_grad, small[2], small[3], small[4], expand_grad,
            small[5:9].reshape(-1), contract_grad, small[9], small[10], small[11])


def solution(mesh):
    data = P("dp", "blk", None)
    in_specs = (data, P("dp"), P("dp", "blk"), P("dp")) + (P(),) * 12 + (data,)
    out_specs = (data, data) + (P(),) * 12
    return jax.shard_map(local, mesh=mesh, in_specs=in_specs, out_specs=out_specs, check_vma=False)
```

```python
import functools

import jax
import jax.numpy as jnp
from jax import lax
from jax.experimental import pallas as pl
from jax.experimental.pallas import tpu as pltpu
from jax.sharding import PartitionSpec as P

D = 768
FF = 3072
HEADS = 12
HEAD_DIM = 64
DOC_SHORT = 128
MESH = pl.DeviceIdType.MESH
EPS = 1e-05
NEG = -1e9
F32, B16 = jnp.float32, jnp.bfloat16
NN = (((1,), (0,)), ((), ()))
NT = (((1,), (1,)), ((), ()))
TN = (((0,), (0,)), ((), ()))

FB = 512
BR, BC = 384, 384
HR = BR // 2
SR = HR // 4
ACROSS = (D // BC, FF // BC, D // BC, 3 * D // BC)
DOWN = (FF // BR, D // BR, D // BR, D // BR)
FROM = [0]
for _down, _across in zip(DOWN, ACROSS):
    FROM.append(FROM[-1] + _down * _across)
N = FROM[-1] // 2
L_AT = (0, FF, FF + D, FF + 2 * D, FF + 3 * D)
R_AT = (0, D, D + FF, 2 * D + FF, 5 * D + FF)
KINDS = 9
CORE, FIRST, SECOND, ZA, ZB, ZC, BACK, AGF, AGC = range(KINDS)
RING = 8
PHASES = 2
OFF = [0, 2, 8, 12, 16, 20, 24, 28, 34, 36]
SMALL = [17 + 3 * i for i in range(7)]
SIDE = ((0, 6, "feed"), (6, 1, "norm"), (7, 6, "attend"), (13, 1, "sums"), (14, 4, "tokens"))
VECS = 16


def dot(a, b, dims=NN):
    return lax.dot_general(a, b, dims, preferred_element_type=F32)


def rows(start, n):
    return pl.ds(pl.multiple_of(start, 16), n)


def cols(start, n):
    return pl.ds(pl.multiple_of(start, 128), n)


def normal_parts(v):
    t = 1.0 / (1.0 + (0.3275911 * 0.5 ** 0.5) * jnp.abs(v))
    ex = jnp.exp(-0.5 * (v * v))
    poly = t * (0.127414796 + t * (-0.142248368 + t * (0.7107068705 + t * (-0.7265760135 + t * 0.5307027145))))
    tail = poly * ex
    below = jnp.where(v < 0, tail, 1.0 - tail)
    return v * below, below + v * (ex * 0.3989422804014327)


def mean(a):
    return jnp.sum(a, axis=1, keepdims=True) * (1.0 / D)


def layer_kernel(kinds, keeps, proj_bias, mix_bias, attn_gain, attn_shift, expand_bias, contract_bias, ffn_gain, ffn_shift,
                 live, tokens, cot_in, w_proj, w_mix, w_exp, w_con,
                 g_out, small_out, out_l, out_t,
                 vecs, wproj, wmix, wexp, wcon, left, right, cot, livebuf, probs, xhat, dres, d_att,
                 send, rstd, bias, held, ebuf,
                 part, r0, r1, za, zb, zc, sm, smr,
                 ssem, rsem, lsem, smss, smrs, wsem, dsend, drecv, dloc):
    dp, z = lax.axis_index("dp"), lax.axis_index("blk")
    T = left.shape[0]
    act, low, att, row = (left.at[:, a:b] for a, b in zip(L_AT, L_AT[1:]))
    d_ffn, gp, d_attn, qkv = (right.at[:, a:b] for a, b in zip(R_AT, R_AT[1:]))
    BL = T // 4
    c, x, y = dp % 2, (dp // 2) % 2, (dp // 4) % 2
    d_core = (dp + 1 - 2 * c, z)
    d_x = (dp + 2 - 4 * x, z)
    d_y = (dp + 4 - 8 * y, z)
    is0, is1 = z == 0, z == 1
    end, mid = (z == 0) | (z == 3), (z == 1) | (z == 2)
    others = (z, z + 1 - 2 * (z % 2), z + 2 - 4 * (z // 2), 3 - z)

    loads = [pltpu.make_async_copy(a, b, wsem.at[i]) for i, (a, b) in
             enumerate(((w_proj, wproj), (w_mix, wmix), (w_exp, wexp), (w_con, wcon)))]

    barrier = pltpu.get_barrier_semaphore()
    for d in (d_core, d_x, d_y) + tuple((dp, others[m]) for m in (1, 2, 3)):
        pl.semaphore_signal(barrier, inc=1, device_id=d, device_id_type=MESH)
    pl.semaphore_wait(barrier, 6)

    TOK, LIVE, COT, OUTL, OUTT = range(5)

    def deal(kind, m, arriving=False):
        there = others[m]
        src, dst = {
            TOK: lambda: (tokens.at[there], row.at[rows((there if arriving else z) * BL, BL)]),
            LIVE: lambda: (live, livebuf.at[there if arriving else z]),
            COT: lambda: (cot_in.at[there], cot.at[rows((there if arriving else z) * BL, BL)]),
            OUTL: lambda: (send.at[rows(there * BL, BL)], out_l.at[there if arriving else z]),
            OUTT: lambda: (send.at[rows(there * BL, BL)], out_t.at[there if arriving else z]),
        }[kind]()
        if m == 0:
            return pltpu.make_async_copy(src, dst, dloc.at[kind])
        return pltpu.make_async_remote_copy(src_ref=src, dst_ref=dst, send_sem=dsend.at[kind, m], recv_sem=drecv.at[kind, m],
                                            device_id=(dp, there), device_id_type=MESH)

    def finish(kind):
        for m in (1, 2, 3):
            deal(kind, m).wait_send()

    for m in (3, 2, 1, 0):
        deal(LIVE, m).start()
        deal(TOK, m).start()
    for load in loads:
        load.start()
    wide = lambda v: v[...].astype(F32).reshape(1, v.shape[0])
    vecs[0:1] = proj_bias[0:1].astype(F32)
    vecs[1:2] = jnp.zeros((1, D), F32)
    vecs[2:3] = proj_bias[1:2].astype(F32)
    for i, v in enumerate((mix_bias, attn_gain, attn_shift, contract_bias, ffn_gain, ffn_shift)):
        vecs[3 + i:4 + i] = wide(v)
    ebias = wide(expand_bias)
    for j in range(FF // FB):
        ebuf[j] = ebias[:, j * FB:(j + 1) * FB]

    def project(m):
        (deal(TOK, 0).wait if m == 0 else deal(TOK, m, True).wait_recv)()
        r = rows(others[m] * BL, BL)
        for j in range(3):
            s = slice(j * D, (j + 1) * D)
            part_j = dot(row[r], wproj[:, s]) + vecs[j:j + 1]
            if j == 0:
                part_j = part_j.astype(B16).astype(F32) * HEAD_DIM ** -0.5
            qkv[r, s] = part_j.astype(B16)

    loads[0].wait()
    for m in (0, 1, 2, 3):
        project(m)
    for m in (3, 2, 1, 0):
        deal(COT, m).start()

    deal(LIVE, 0).wait()
    for m in (1, 2, 3):
        deal(LIVE, m, True).wait_recv()
    count = jnp.sum(sum(livebuf[j, pl.ds(z, 1)] for j in range(4)), axis=1, keepdims=True)
    short = (1 - kinds[z]).astype(F32) * NEG
    for b in range(4):
        key = lax.broadcasted_iota(jnp.int32, (BL, T), 0) + b * BL
        query = lax.broadcasted_iota(jnp.int32, (BL, T), 1)
        shift = DOC_SHORT.bit_length() - 1
        apart = jnp.where((key >> shift) == (query >> shift), 0.0, short)
        bias[b * BL:(b + 1) * BL] = jnp.where(key < count, apart, NEG)

    def attend(i, _):
        s = cols(i * 2 * HEAD_DIM, 2 * HEAD_DIM)
        q2, k2, v2 = (qkv[:, cols(j * D + i * 2 * HEAD_DIM, 2 * HEAD_DIM)] for j in range(3))
        outs = []
        for h in range(2):
            hs = slice(h * HEAD_DIM, (h + 1) * HEAD_DIM)
            scores = dot(k2[:, hs], q2[:, hs], NT) + bias[...]
            e = jnp.exp(scores - jnp.max(scores, axis=0, keepdims=True))
            p = (e * (1.0 / jnp.sum(e, axis=0, keepdims=True))).astype(B16)
            probs[2 * i + h] = p
            outs.append(dot(v2[:, hs], p, TN))
        att[:, s] = jnp.concatenate(outs, axis=0).T.astype(B16)
        return 0
    lax.fori_loop(0, HEADS // 2, attend, 0)

    loads[1].wait()
    RB = 256

    def norm_one(i, _):
        r = rows(i * RB, RB)
        h = row[r].astype(F32) + (dot(att[r], wmix[...]) + vecs[3:4])
        h = h - mean(h)
        rs = lax.rsqrt(mean(h * h) + EPS)
        h = h * rs
        xhat[r] = h
        rstd[r] = rs
        low[r] = (h * vecs[4:5] + vecs[5:6]).astype(B16)
        return 0
    lax.fori_loop(0, T // RB, norm_one, 0)

    loads[2].wait()
    loads[3].wait()
    dres[...] = jnp.zeros_like(dres)

    def feed(j, _):
        s = cols(j * FB, FB)
        pre = dot(low[...], wexp[:, s]) + ebuf[j]
        value, slope = normal_parts(pre)
        value = value.astype(B16)
        act[:, s] = value
        gp[:, s] = slope.astype(B16)
        dres[...] += dot(value, wcon[rows(j * FB, FB)])
        return 0
    lax.fori_loop(0, FF // FB, feed, 0)

    keep = keeps[z].astype(F32)
    for kind in (COT,):
        deal(kind, 0).wait()
        for m in (1, 2, 3):
            deal(kind, m, True).wait_recv()
    sm[0] = jnp.zeros((VECS, D), F32)

    def norm_two(i, _):
        r = rows(i * BL, BL)
        h = (xhat[r] * vecs[4:5] + vecs[5:6]) + (dres[r] + vecs[6:7])
        h = h - mean(h)
        rs = lax.rsqrt(mean(h * h) + EPS)
        h = h * rs
        send[r] = jnp.where(keep > 0, h * vecs[7:8] + vecs[8:9], row[r].astype(F32)).astype(B16)
        grad = cot[r].astype(F32) * keep
        sm[0, 10:11] += jnp.sum(grad * h, axis=0, keepdims=True)
        sm[0, 11:12] += jnp.sum(grad, axis=0, keepdims=True)
        dx = grad * vecs[7:8]
        dr = rs * (dx - mean(dx) - h * mean(dx * h))
        dres[r] = dr
        dr = dr.astype(B16)
        d_ffn[r] = dr
        sm[0, 9:10] += jnp.sum(dr.astype(F32), axis=0, keepdims=True)
        return 0
    lax.fori_loop(0, T // BL, norm_two, 0)
    for m in (3, 2, 1, 0):
        deal(OUTL, m).start()

    def back_feed(j, step):
        s = cols(j * FB, FB)
        if step == 0:
            gp[:, s] = (dot(d_ffn[...], wcon[rows(j * FB, FB)], NT) * gp[:, s].astype(F32)).astype(B16)
        else:
            dres[...] += dot(gp[:, s], wexp[:, s], NT)

    def back_norm(_, step):
        if step == 1:
            d_att[...] = dot(d_attn[...], wmix[...], NT).astype(B16)
            return
        for q in range(FF // D):
            sm[0, 5 + q:6 + q] = jnp.sum(gp[:, q * D:(q + 1) * D].astype(F32), axis=0, keepdims=True)

        def block(i, _):
            r = rows(i * BL, BL)
            dn, h = dres[r], xhat[r]
            sm[0, 3:4] += jnp.sum(dn * h, axis=0, keepdims=True)
            sm[0, 4:5] += jnp.sum(dn, axis=0, keepdims=True)
            dx = dn * vecs[4:5]
            dr = rstd[r] * (dx - mean(dx) - h * mean(dx * h))
            dres[r] = dr
            dr = dr.astype(B16)
            d_attn[r] = dr
            sm[0, 2:3] += jnp.sum(dr.astype(F32), axis=0, keepdims=True)
            return 0
        lax.fori_loop(0, T // BL, block, 0)

    def back_attend(i, step):
        at = [cols(j * D + i * 2 * HEAD_DIM, 2 * HEAD_DIM) for j in range(3)]
        hs = slice(step * HEAD_DIM, (step + 1) * HEAD_DIM)
        q1, k1, v1 = (qkv[:, s][:, hs] for s in at)
        da1 = d_att[:, at[0]][:, hs]
        p = probs[2 * i + step]
        dp_t = dot(v1, da1, NT)
        pf = p.astype(F32)
        delta = jnp.sum(pf * dp_t, axis=0, keepdims=True)
        ds = (pf * (dp_t - delta)).astype(B16)
        dq = (dot(k1, ds, TN) * HEAD_DIM ** -0.5).T
        dk, dv = dot(ds, q1), dot(p, da1)
        for j, d in enumerate((dq, dk, dv)):
            if step == 0:
                held[j] = d.astype(B16)
            else:
                qkv[:, at[j]] = jnp.concatenate([held[j], d.astype(B16)], axis=1)

    def back_sums(_, step):
        if step:
            return
        sm[0, 0:1] = jnp.sum(qkv[:, 0:D].astype(F32), axis=0, keepdims=True)
        sm[0, 1:2] = jnp.sum(qkv[:, 2 * D:].astype(F32), axis=0, keepdims=True)

    def back_tokens(i, step):
        for m in range(4) if step == 0 else ():
            @pl.when(i == m)
            def _():
                if m == 0:
                    deal(OUTL, 0).wait()
                    finish(OUTL)
                r = rows(others[m] * BL, BL)
                d = dres[r] + dot(qkv[r], wproj[...], NT)
                send[r] = jnp.where(keep > 0, d, cot[r].astype(F32)).astype(B16)
                deal(OUTT, m).start()

    def cp(kind, k, src, dst, dev):
        return pltpu.make_async_remote_copy(src_ref=src, dst_ref=dst, send_sem=ssem.at[kind, k % RING],
                                            recv_sem=rsem.at[kind, k % RING], device_id=dev, device_id_type=MESH)

    def way(k):
        par = k % 2
        f = x * (1 - par) + y * par
        d_first = (dp + (1 - par) * (2 - 4 * x) + par * (4 - 8 * y), z)
        d_last = (dp + par * (2 - 4 * x) + (1 - par) * (4 - 8 * y), z)
        return f, d_first, d_last

    def c_core(k):
        return cp(CORE, k, part.at[k % 2, 1 - c], r0.at[k], d_core)

    def c_first(k):
        f, d_first, _ = way(k)
        return cp(FIRST, k, r0.at[k, rows((1 - f) * HR, HR)], r1.at[k], d_first)

    def place(k, shard, n=1):
        f, _, _ = way(k)
        return g_out.at[2 * k + c, rows(f * HR + shard * SR, n * SR)]

    def half(k):
        par = k % 2
        return y * (1 - par) + x * par

    def own_half(k):
        return rows(half(k) * 2 * SR, 2 * SR)

    def f_second(k):
        _, _, d_last = way(k)
        return cp(SECOND, k, r1.at[k, rows((1 - half(k)) * 2 * SR, 2 * SR)], za.at[k], d_last)

    def f_za(k):
        return cp(ZA, k, r1.at[k, own_half(k)], zb.at[k], (dp, jnp.where(is0, 1, 2)))

    def f_zb(k):
        return cp(ZB, k, r1.at[k, own_half(k)], zc.at[k], (dp, jnp.where(is1, 2, 1)))

    def f_place(k):
        return place(k, 2 * half(k), 2)

    def f_zc(k):
        return cp(ZC, k, za.at[k], f_place(k), (dp, jnp.where(is1, 0, 3)))

    def f_own(k):
        return pltpu.make_async_copy(za.at[k], f_place(k), lsem.at[k % RING])

    def f_back(k, from_place):
        _, _, d_last = way(k)
        return cp(BACK, k, f_place(k) if from_place else za.at[k], f_place(k), d_last)

    def f_back_in(k):
        _, _, d_last = way(k)
        there = place(k, 2 * (1 - half(k)), 2)
        return cp(BACK, k, there, there, d_last)

    def c_agf(k):
        f, d_first, _ = way(k)
        block = g_out.at[2 * k + c, rows(f * HR, HR)]
        return cp(AGF, k, block, block, d_first)

    def c_agc(k):
        block = g_out.at[2 * k + c]
        return cp(AGC, k, block, block, d_core)

    def add(a, b):
        return (a.astype(F32) + b.astype(F32)).astype(B16)

    def produce(k):
        l, r = 0, 0
        for first, across, la, ra in zip(FROM, ACROSS, L_AT, R_AT):
            at = 2 * k - first
            l = jnp.where(at >= 0, la + at // across * BR, l)
            r = jnp.where(at >= 0, ra + at % across * BC, r)
        both = dot(left[:, cols(l, BR)], right[:, cols(r, 2 * BC)], TN).astype(B16)
        for i in range(2):
            part[k % 2, i] = both[:, i * BC:(i + 1) * BC]

    def stage(s, k):
        f, _, _ = way(k)
        if s == 0:
            produce(k)
            c_core(k).start()
        elif s == 1:
            c_core(k).wait()
            r0[k] = add(r0[k], part[k % 2, c])
            c_first(k).start()
        elif s == 2:
            c_first(k).wait()
            r1[k] = add(r1[k], r0[k, rows(f * HR, HR)])
            f_second(k).start()
        elif s == 3:
            f_second(k).wait()
            r1[k, own_half(k)] = add(r1[k, own_half(k)], za[k])

            @pl.when(end)
            def _():
                f_za(k).start()
        elif s == 4:
            @pl.when(mid)
            def _():
                f_za(k).wait_recv()
                r1[k, own_half(k)] = add(r1[k, own_half(k)], zb[k])
                f_zb(k).start()
        elif s == 5:
            @pl.when(mid)
            def _():
                f_zb(k).wait()
                za[k] = add(r1[k, own_half(k)], zc[k])
                f_zc(k).start()
                f_back(k, False).start()
                f_own(k).start()
        elif s == 6:
            @pl.when(end)
            def _():
                f_zc(k).wait_recv()
                f_back(k, True).start()
                f_za(k).wait_send()
        elif s == 7:
            f_back_in(k).wait_recv()
            f_back(k, True).wait_send()

            @pl.when(mid)
            def _():
                f_own(k).wait()
                f_zc(k).wait_send()
            c_agf(k).start()
        elif s == 8:
            c_agf(k).wait()
            c_agc(k).start()
        elif s == 9:
            c_agc(k).wait()

    steps = ((d_core, None, None), (d_x, None, None), (d_y, None, None),
             ((dp, jnp.where(is0, 1, 2)), end, mid), ((dp, jnp.where(is1, 2, 1)), mid, mid), ((dp, jnp.where(is1, 0, 3)), mid, end))

    def only(cond, f):
        f() if cond is None else pl.when(cond)(f)

    def s_copy(i):
        return pltpu.make_async_remote_copy(src_ref=sm.at[i], dst_ref=smr.at[i], send_sem=smss.at[i], recv_sem=smrs.at[i],
                                            device_id=steps[i][0], device_id_type=MESH)

    def small_step(i):
        if i > 0:
            sm[i] = sm[i - 1]

            def get():
                s_copy(i - 1).wait_recv()
                sm[i] = smr[i - 1] if i == 6 else sm[i - 1] + smr[i - 1]
            only(steps[i - 1][2], get)
        if i < 6:
            only(steps[i][1], lambda: s_copy(i).start())

    def tick(t, _):
        works = {"feed": back_feed, "norm": back_norm, "attend": back_attend, "sums": back_sums, "tokens": back_tokens}
        for phase in range(PHASES):
            for s in range(len(OFF) - 1, -1, -1):
                if OFF[s] % PHASES == phase:
                    k = t - OFF[s] // PHASES

                    @pl.when((k >= 0) & (k < N))
                    def _():
                        stage(s, k)
            for step in range(phase * 2 // PHASES, (phase + 1) * 2 // PHASES):
                for first, count, work in SIDE:
                    @pl.when((t >= first) & (t < first + count))
                    def _():
                        works[work](t - first, step)
        for i in range(7):
            @pl.when(t == SMALL[i])
            def _():
                small_step(i)
        return 0
    lax.fori_loop(0, N + OFF[-1] // PHASES, tick, 0)

    small_out[...] = sm[6]
    for i in range(6):
        only(steps[i][1], lambda: s_copy(i).wait_send())
    deal(OUTT, 0).wait()
    for kind in (TOK, LIVE, COT, OUTT):
        finish(kind)
    for m in (1, 2, 3):
        deal(OUTL, m, True).wait_recv()
        deal(OUTT, m, True).wait_recv()


def run_layer(kinds, keeps, *rest):
    tokens = rest[9]
    blocks, BL, _ = tokens.shape
    T = blocks * BL
    V, S, H = (pl.BlockSpec(memory_space=m) for m in (pltpu.VMEM, pltpu.SMEM, pltpu.HBM))
    low16 = lambda *s: pltpu.VMEM(s, B16)
    full = lambda *s: pltpu.VMEM(s, F32)
    sem = lambda *s: pltpu.SemaphoreType.DMA(s)
    return pl.pallas_call(
        layer_kernel,
        out_shape=[jax.ShapeDtypeStruct((2 * N, BR, BC), B16), jax.ShapeDtypeStruct((VECS, D), F32),
                   jax.ShapeDtypeStruct(tokens.shape, B16), jax.ShapeDtypeStruct(tokens.shape, B16)],
        in_specs=[S, S] + [V] * 9 + [H] * 6,
        out_specs=[H, V, H, H],
        scratch_shapes=[
            full(VECS, D), low16(D, 3 * D), low16(D, D), low16(D, FF), low16(FF, D),
            low16(T, L_AT[-1]), low16(T, R_AT[-1]), low16(T, D), pltpu.VMEM((blocks, blocks, BL), jnp.int32), low16(HEADS, T, T),
            full(T, D), full(T, D), low16(T, D),
            low16(T, D), full(T, 1), full(T, T), low16(3, T, HEAD_DIM), full(FF // FB, 1, FB),
            low16(2, 2, BR, BC), low16(N, BR, BC), low16(N, HR, BC), low16(N, 2 * SR, BC), low16(N, 2 * SR, BC),
            low16(N, 2 * SR, BC), full(7, VECS, D), full(6, VECS, D),
            sem(KINDS, RING), sem(KINDS, RING), sem(RING), sem(6), sem(6), sem(4), sem(5, 4), sem(5, 4), sem(5),
        ],
        compiler_params=pltpu.CompilerParams(collective_id=0, has_side_effects=True, vmem_limit_bytes=63 * 2**20),
        name="layer",
    )(kinds, keeps, *rest)


AHEAD = 4


def widen_kernel(g, small, out_l, out_t, layer_out, tokens_grad, projection, proj_bias, mixing, mix_bias, attn_gain, attn_shift,
                 expand, expand_bias, contract, contract_bias, ffn_gain, ffn_shift, low, wide, tin, tout, lin, isem, osem, tsem):
    def come(k):
        return pltpu.make_async_copy(g.at[pl.ds(2 * k, 2)], low.at[k], isem.at[k])

    def go(k, ref, at, across):
        return pltpu.make_async_copy(wide.at[k], ref.at[rows(at // across * BR, BR), cols(at % across * 2 * BC, 2 * BC)], osem.at[k])

    t_in, t_out = pltpu.make_async_copy(out_t, tin, tsem.at[0]), pltpu.make_async_copy(tout, tokens_grad, tsem.at[1])
    l_in, l_out = pltpu.make_async_copy(out_l, lin, tsem.at[2]), pltpu.make_async_copy(lin, layer_out, tsem.at[3])
    t_in.start()
    l_in.start()
    for k in range(AHEAD):
        come(k).start()
    grads = list(zip((contract, expand, mixing, projection), FROM, FROM[1:], ACROSS))
    for ref, first, last, across in grads:
        def step(k, _):
            @pl.when(k + AHEAD < N)
            def _():
                come(k + AHEAD).start()
            come(k).wait()
            for i in range(2):
                wide[k, :, i * BC:(i + 1) * BC] = low[k, i].astype(F32)
            go(k, ref, k - first // 2, across // 2).start()
            return 0
        lax.fori_loop(first // 2, last // 2, step, 0)
    l_in.wait()
    l_out.start()
    t_in.wait()
    tout[...] = tin[...].astype(F32)
    t_out.start()
    proj_bias[...] = small[0:2]
    for i, ref in ((2, mix_bias), (3, attn_gain), (4, attn_shift), (9, contract_bias), (10, ffn_gain), (11, ffn_shift)):
        ref[...] = small[i:i + 1].reshape(D)
    for q in range(FF // D):
        expand_bias[q * D:(q + 1) * D] = small[5 + q:6 + q].reshape(D)
    l_out.wait()
    t_out.wait()
    for ref, first, last, across in grads:
        def done(k, _):
            go(k, ref, k - first // 2, across // 2).wait()
            return 0
        lax.fori_loop(first // 2, last // 2, done, 0)


def widen(g, small, out_l, out_t):
    V, H = (pl.BlockSpec(memory_space=m) for m in (pltpu.VMEM, pltpu.HBM))
    shape = lambda *s: jax.ShapeDtypeStruct(s, F32)
    vec = shape(D)
    return pl.pallas_call(
        widen_kernel,
        in_specs=[H, V, H, H],
        out_specs=[H, H, H, V, H, V, V, V, H, V, H, V, V, V],
        out_shape=[jax.ShapeDtypeStruct(out_l.shape, B16), shape(*out_t.shape), shape(D, 3 * D), shape(2, D), shape(D, D),
                   vec, vec, vec, shape(D, FF), shape(FF), shape(FF, D), vec, vec, vec],
        scratch_shapes=[pltpu.VMEM((N, 2, BR, BC), B16), pltpu.VMEM((N, BR, 2 * BC), F32), pltpu.VMEM(out_t.shape, B16),
                        pltpu.VMEM(out_t.shape, F32), pltpu.VMEM(out_l.shape, B16)] + [pltpu.SemaphoreType.DMA((n,)) for n in (N, N, 4)],
        compiler_params=pltpu.CompilerParams(vmem_limit_bytes=60 * 2**20),
        cost_estimate=pl.CostEstimate(flops=0, bytes_accessed=12 * N * BR * BC, transcendentals=0),
        name="widen",
    )(g, small, out_l, out_t)


def local(tokens, row_kinds, live_mask, keep_flag, projection, proj_bias, mixing, mix_bias, attn_gain, attn_shift,
          expand, expand_bias, contract, contract_bias, ffn_gain, ffn_shift, cotangent):
    g, small, layer_out, tokens_grad = run_layer(
        row_kinds, keep_flag, proj_bias, mix_bias, attn_gain, attn_shift, expand_bias, contract_bias, ffn_gain, ffn_shift,
        live_mask, tokens, cotangent, projection, mixing, expand, contract)
    groups = lax.axis_size("dp") // 8
    if groups > 1:
        index = [[i + 8 * j for j in range(groups)] for i in range(8)]
        g, small = lax.psum((g, small), "dp", axis_index_groups=index)
    return tuple(widen(g, small, layer_out, tokens_grad))


def solution(mesh):
    data = P("dp", "blk", None)
    in_specs = (data, P("dp"), P("dp", "blk"), P("dp")) + (P(),) * 12 + (data,)
    out_specs = (data, data) + (P(),) * 12
    return jax.shard_map(local, mesh=mesh, in_specs=in_specs, out_specs=out_specs, check_vma=False)
```

```python
import functools

import jax
import jax.numpy as jnp
from jax import lax
from jax.experimental import pallas as pl
from jax.experimental.pallas import tpu as pltpu
from jax.sharding import PartitionSpec as P

D = 768
FF = 3072
HEADS = 12
HEAD_DIM = 64
DOC_SHORT = 128
MESH = pl.DeviceIdType.MESH
EPS = 1e-05
NEG = -1e9
F32, B16 = jnp.float32, jnp.bfloat16
NN = (((1,), (0,)), ((), ()))
NT = (((1,), (1,)), ((), ()))
TN = (((0,), (0,)), ((), ()))

FB = 512
BR, BC = 384, 384
HR = BR // 2
SR = HR // 4
ACROSS = (D // BC, FF // BC, D // BC, 3 * D // BC)
DOWN = (FF // BR, D // BR, D // BR, D // BR)
FROM = [0]
for _down, _across in zip(DOWN, ACROSS):
    FROM.append(FROM[-1] + _down * _across)
N = FROM[-1] // 2
L_AT = (0, FF, FF + D, FF + 2 * D, FF + 3 * D)
R_AT = (0, D, D + FF, 2 * D + FF, 5 * D + FF)
KINDS = 15
CORE, FIRST, SECOND, ZA, ZB, ZC, BACK, AGF, AGC, MID, TOEND, I_ZA, I_ZB, I_ZC, I_SECOND = range(KINDS)
INNER = (10, 18)
RING = 8
PHASES = 2
OFF = [0, 2, 8, 12, 16, 20, 24, 28, 34, 38]
OFF_INNER = [0, 2, 8, 13, 17, 21, 25, 29, 35, 39]
SMALL = [17 + 3 * i for i in range(7)]
SIDE = ((0, 6, "feed"), (6, 1, "norm"), (7, 6, "attend"), (13, 1, "sums"), (14, 4, "tokens"))
VECS = 16


def dot(a, b, dims=NN):
    return lax.dot_general(a, b, dims, preferred_element_type=F32)


def rows(start, n):
    return pl.ds(pl.multiple_of(start, 16), n)


def cols(start, n):
    return pl.ds(pl.multiple_of(start, 128), n)


def normal_parts(v):
    t = 1.0 / (1.0 + (0.3275911 * 0.5 ** 0.5) * jnp.abs(v))
    ex = jnp.exp(-0.5 * (v * v))
    poly = t * (0.127414796 + t * (-0.142248368 + t * (0.7107068705 + t * (-0.7265760135 + t * 0.5307027145))))
    tail = poly * ex
    below = jnp.where(v < 0, tail, 1.0 - tail)
    return v * below, below + v * (ex * 0.3989422804014327)


def mean(a):
    return jnp.sum(a, axis=1, keepdims=True) * (1.0 / D)


def layer_kernel(kinds, keeps, proj_bias, mix_bias, attn_gain, attn_shift, expand_bias, contract_bias, ffn_gain, ffn_shift,
                 live, tokens, cot_in, w_proj, w_mix, w_exp, w_con,
                 g_out, small_out, out_l, out_t,
                 vecs, wproj, wmix, wexp, wcon, left, right, cot, livebuf, probs, xhat, dres, d_att,
                 send, rstd, bias, held, ebuf,
                 part, r0, r1, za, zb, zc, sm, smr,
                 ssem, rsem, lsem, smss, smrs, wsem, dsend, drecv, dloc):
    dp, z = lax.axis_index("dp"), lax.axis_index("blk")
    T = left.shape[0]
    act, low, att, row = (left.at[:, a:b] for a, b in zip(L_AT, L_AT[1:]))
    d_ffn, gp, d_attn, qkv = (right.at[:, a:b] for a, b in zip(R_AT, R_AT[1:]))
    BL = T // 4
    c, x, y = dp % 2, (dp // 2) % 2, (dp // 4) % 2
    d_core = (dp + 1 - 2 * c, z)
    d_x = (dp + 2 - 4 * x, z)
    d_y = (dp + 4 - 8 * y, z)
    is0, is1 = z == 0, z == 1
    end, mid = (z == 0) | (z == 3), (z == 1) | (z == 2)
    others = (z, z + 1 - 2 * (z % 2), z + 2 - 4 * (z // 2), 3 - z)

    loads = [pltpu.make_async_copy(a, b, wsem.at[i]) for i, (a, b) in
             enumerate(((w_proj, wproj), (w_mix, wmix), (w_exp, wexp), (w_con, wcon)))]

    barrier = pltpu.get_barrier_semaphore()
    for d in (d_core, d_x, d_y) + tuple((dp, others[m]) for m in (1, 2, 3)):
        pl.semaphore_signal(barrier, inc=1, device_id=d, device_id_type=MESH)
    pl.semaphore_wait(barrier, 6)

    TOK, LIVE, COT, OUTL, OUTT = range(5)

    def deal(kind, m, arriving=False):
        there = others[m]
        src, dst = {
            TOK: lambda: (tokens.at[there], row.at[rows((there if arriving else z) * BL, BL)]),
            LIVE: lambda: (live, livebuf.at[there if arriving else z]),
            COT: lambda: (cot_in.at[there], cot.at[rows((there if arriving else z) * BL, BL)]),
            OUTL: lambda: (send.at[rows(there * BL, BL)], out_l.at[there if arriving else z]),
            OUTT: lambda: (send.at[rows(there * BL, BL)], out_t.at[there if arriving else z]),
        }[kind]()
        if m == 0:
            return pltpu.make_async_copy(src, dst, dloc.at[kind])
        return pltpu.make_async_remote_copy(src_ref=src, dst_ref=dst, send_sem=dsend.at[kind, m], recv_sem=drecv.at[kind, m],
                                            device_id=(dp, there), device_id_type=MESH)

    def finish(kind):
        for m in (1, 2, 3):
            deal(kind, m).wait_send()

    for m in (3, 2, 1, 0):
        deal(LIVE, m).start()
        deal(TOK, m).start()
    for load in loads:
        load.start()
    wide = lambda v: v[...].astype(F32).reshape(1, v.shape[0])
    vecs[0:1] = proj_bias[0:1].astype(F32)
    vecs[1:2] = jnp.zeros((1, D), F32)
    vecs[2:3] = proj_bias[1:2].astype(F32)
    for i, v in enumerate((mix_bias, attn_gain, attn_shift, contract_bias, ffn_gain, ffn_shift)):
        vecs[3 + i:4 + i] = wide(v)
    ebias = wide(expand_bias)
    for j in range(FF // FB):
        ebuf[j] = ebias[:, j * FB:(j + 1) * FB]

    def project(m):
        (deal(TOK, 0).wait if m == 0 else deal(TOK, m, True).wait_recv)()
        r = rows(others[m] * BL, BL)
        for j in range(3):
            s = slice(j * D, (j + 1) * D)
            part_j = dot(row[r], wproj[:, s]) + vecs[j:j + 1]
            if j == 0:
                part_j = part_j.astype(B16).astype(F32) * HEAD_DIM ** -0.5
            qkv[r, s] = part_j.astype(B16)

    loads[0].wait()
    for m in (0, 1, 2, 3):
        project(m)
    for m in (3, 2, 1, 0):
        deal(COT, m).start()

    deal(LIVE, 0).wait()
    for m in (1, 2, 3):
        deal(LIVE, m, True).wait_recv()
    count = jnp.sum(sum(livebuf[j, pl.ds(z, 1)] for j in range(4)), axis=1, keepdims=True)
    short = (1 - kinds[z]).astype(F32) * NEG
    for b in range(4):
        key = lax.broadcasted_iota(jnp.int32, (BL, T), 0) + b * BL
        query = lax.broadcasted_iota(jnp.int32, (BL, T), 1)
        shift = DOC_SHORT.bit_length() - 1
        apart = jnp.where((key >> shift) == (query >> shift), 0.0, short)
        bias[b * BL:(b + 1) * BL] = jnp.where(key < count, apart, NEG)

    def attend_pair(i):
        s = cols(i * 2 * HEAD_DIM, 2 * HEAD_DIM)
        q2, k2, v2 = (qkv[:, cols(j * D + i * 2 * HEAD_DIM, 2 * HEAD_DIM)] for j in range(3))
        outs = []
        for h in range(2):
            hs = slice(h * HEAD_DIM, (h + 1) * HEAD_DIM)
            scores = dot(k2[:, hs], q2[:, hs], NT) + bias[...]
            e = jnp.exp(scores - jnp.max(scores, axis=0, keepdims=True))
            p = (e * (1.0 / jnp.sum(e, axis=0, keepdims=True))).astype(B16)
            probs[2 * i + h] = p
            outs.append(dot(v2[:, hs], p, TN))
        att[:, s] = jnp.concatenate(outs, axis=0).T.astype(B16)
    def attend(i, _):
        for j in range(2):
            attend_pair(i * 2 + j)
        return 0
    lax.fori_loop(0, HEADS // 4, attend, 0)

    loads[1].wait()
    RB = 256

    def norm_one(i, _):
        r = rows(i * RB, RB)
        h = row[r].astype(F32) + (dot(att[r], wmix[...]) + vecs[3:4])
        h = h - mean(h)
        rs = lax.rsqrt(mean(h * h) + EPS)
        h = h * rs
        xhat[r] = h
        rstd[r] = rs
        low[r] = (h * vecs[4:5] + vecs[5:6]).astype(B16)
        return 0
    lax.fori_loop(0, T // RB, norm_one, 0)

    loads[2].wait()
    loads[3].wait()
    dres[...] = jnp.zeros_like(dres)

    def feed(j, _):
        s = cols(j * FB, FB)
        parts = [slice(i * T // 2, (i + 1) * T // 2) for i in range(2)]
        pres = [dot(low[p, :], wexp[:, s]) + ebuf[j] for p in parts]
        for p, pre in zip(parts, pres):
            value, slope = normal_parts(pre)
            value = value.astype(B16)
            act[p, s] = value
            gp[p, s] = slope.astype(B16)
            dres[p, :] += dot(value, wcon[rows(j * FB, FB)])
        return 0
    lax.fori_loop(0, FF // FB, feed, 0)

    keep = keeps[z].astype(F32)
    for kind in (COT,):
        deal(kind, 0).wait()
        for m in (1, 2, 3):
            deal(kind, m, True).wait_recv()
    sm[0] = jnp.zeros((VECS, D), F32)

    def norm_two(i, _):
        r = rows(i * BL, BL)
        h = (xhat[r] * vecs[4:5] + vecs[5:6]) + (dres[r] + vecs[6:7])
        h = h - mean(h)
        rs = lax.rsqrt(mean(h * h) + EPS)
        h = h * rs
        send[r] = jnp.where(keep > 0, h * vecs[7:8] + vecs[8:9], row[r].astype(F32)).astype(B16)
        grad = cot[r].astype(F32) * keep
        sm[0, 10:11] += jnp.sum(grad * h, axis=0, keepdims=True)
        sm[0, 11:12] += jnp.sum(grad, axis=0, keepdims=True)
        dx = grad * vecs[7:8]
        dr = rs * (dx - mean(dx) - h * mean(dx * h))
        dres[r] = dr
        dr = dr.astype(B16)
        d_ffn[r] = dr
        sm[0, 9:10] += jnp.sum(dr.astype(F32), axis=0, keepdims=True)
        return 0
    lax.fori_loop(0, T // BL, norm_two, 0)
    for m in (3, 2, 1, 0):
        deal(OUTL, m).start()

    def back_feed(j, step):
        s = cols(j * FB, FB)
        if step == 0:
            gp[:, s] = (dot(d_ffn[...], wcon[rows(j * FB, FB)], NT) * gp[:, s].astype(F32)).astype(B16)
        else:
            dres[...] += dot(gp[:, s], wexp[:, s], NT)

    def back_norm(_, step):
        if step == 1:
            d_att[...] = dot(d_attn[...], wmix[...], NT).astype(B16)
            return
        for q in range(FF // D):
            sm[0, 5 + q:6 + q] = jnp.sum(gp[:, q * D:(q + 1) * D].astype(F32), axis=0, keepdims=True)

        def block(i, _):
            r = rows(i * BL, BL)
            dn, h = dres[r], xhat[r]
            sm[0, 3:4] += jnp.sum(dn * h, axis=0, keepdims=True)
            sm[0, 4:5] += jnp.sum(dn, axis=0, keepdims=True)
            dx = dn * vecs[4:5]
            dr = rstd[r] * (dx - mean(dx) - h * mean(dx * h))
            dres[r] = dr
            dr = dr.astype(B16)
            d_attn[r] = dr
            sm[0, 2:3] += jnp.sum(dr.astype(F32), axis=0, keepdims=True)
            return 0
        lax.fori_loop(0, T // BL, block, 0)

    def back_attend(i, step):
        at = [cols(j * D + i * 2 * HEAD_DIM, 2 * HEAD_DIM) for j in range(3)]
        hs = slice(step * HEAD_DIM, (step + 1) * HEAD_DIM)
        q1, k1, v1 = (qkv[:, s][:, hs] for s in at)
        da1 = d_att[:, at[0]][:, hs]
        p = probs[2 * i + step]
        dp_t = dot(v1, da1, NT)
        pf = p.astype(F32)
        delta = jnp.sum(pf * dp_t, axis=0, keepdims=True)
        ds = (pf * (dp_t - delta)).astype(B16)
        dq = (dot(k1, ds, TN) * HEAD_DIM ** -0.5).T
        dk, dv = dot(ds, q1), dot(p, da1)
        for j, d in enumerate((dq, dk, dv)):
            if step == 0:
                held[j] = d.astype(B16)
            else:
                qkv[:, at[j]] = jnp.concatenate([held[j], d.astype(B16)], axis=1)

    def back_sums(_, step):
        if step:
            return
        sm[0, 0:1] = jnp.sum(qkv[:, 0:D].astype(F32), axis=0, keepdims=True)
        sm[0, 1:2] = jnp.sum(qkv[:, 2 * D:].astype(F32), axis=0, keepdims=True)

    def back_tokens(i, step):
        for m in range(4) if step == 0 else ():
            @pl.when(i == m)
            def _():
                if m == 0:
                    deal(OUTL, 0).wait()
                    finish(OUTL)
                r = rows(others[m] * BL, BL)
                d = dres[r] + dot(qkv[r], wproj[...], NT)
                send[r] = jnp.where(keep > 0, d, cot[r].astype(F32)).astype(B16)
                deal(OUTT, m).start()

    def cp(kind, k, src, dst, dev):
        return pltpu.make_async_remote_copy(src_ref=src, dst_ref=dst, send_sem=ssem.at[kind, k % RING],
                                            recv_sem=rsem.at[kind, k % RING], device_id=dev, device_id_type=MESH)

    def way(k):
        par = k % 2
        f = x * (1 - par) + y * par
        d_first = (dp + (1 - par) * (2 - 4 * x) + par * (4 - 8 * y), z)
        d_last = (dp + par * (2 - 4 * x) + (1 - par) * (4 - 8 * y), z)
        return f, d_first, d_last

    def c_core(k):
        return cp(CORE, k, part.at[k % 2, 1 - c], r0.at[k], d_core)

    def c_first(k):
        f, d_first, _ = way(k)
        return cp(FIRST, k, r0.at[k, rows((1 - f) * HR, HR)], r1.at[k], d_first)

    def place(k, shard, n=1):
        f, _, _ = way(k)
        return g_out.at[2 * k + c, rows(f * HR + shard * SR, n * SR)]

    def half(k):
        par = k % 2
        return y * (1 - par) + x * par

    def own_half(k):
        return rows(half(k) * 2 * SR, 2 * SR)

    def f_second(k):
        _, _, d_last = way(k)
        return cp(SECOND, k, r1.at[k, rows((1 - half(k)) * 2 * SR, 2 * SR)], za.at[k, rows(0, 2 * SR)], d_last)

    def f_za(k):
        return cp(ZA, k, r1.at[k, own_half(k)], zb.at[k], (dp, jnp.where(is0, 1, 2)))

    def f_zb(k):
        return cp(ZB, k, r1.at[k, own_half(k)], zc.at[k], (dp, jnp.where(is1, 2, 1)))

    def f_place(k):
        return place(k, 2 * half(k), 2)

    def f_zc(k):
        return cp(ZC, k, za.at[k, rows(0, 2 * SR)], f_place(k), (dp, jnp.where(is1, 0, 3)))

    def f_own(k):
        return pltpu.make_async_copy(za.at[k, rows(0, 2 * SR)], f_place(k), lsem.at[k % RING])

    def f_back(k, from_place):
        _, _, d_last = way(k)
        return cp(BACK, k, f_place(k) if from_place else za.at[k, rows(0, 2 * SR)], f_place(k), d_last)

    def f_back_in(k):
        _, _, d_last = way(k)
        there = place(k, 2 * (1 - half(k)), 2)
        return cp(BACK, k, there, there, d_last)

    side = jnp.where(z < 2, 0, 1)
    mine, theirs = rows(side * 2 * SR, 2 * SR), rows((1 - side) * 2 * SR, 2 * SR)

    def i_za(k):
        return cp(I_ZA, k, r1.at[k], za.at[k], (dp, jnp.where(is0, 1, 2)))

    def i_zb(k):
        return cp(I_ZB, k, r1.at[k, theirs], zb.at[k], (dp, jnp.where(is1, 2, 1)))

    def i_second(k):
        _, _, d_last = way(k)
        return cp(I_SECOND, k, r1.at[k, mine], zc.at[k], d_last)

    def i_own(k):
        return pltpu.make_async_copy(za.at[k, rows(0, 2 * SR)], place(k, 2 * side, 2), lsem.at[k % RING])

    def i_mid(k):
        return cp(MID, k, za.at[k, rows(0, 2 * SR)], place(k, 2 * side, 2), (dp, jnp.where(is1, 2, 1)))

    def i_end(k):
        return cp(I_ZC, k, za.at[k, rows(0, 2 * SR)], place(k, 2 * side, 2), (dp, jnp.where(is1, 0, 3)))

    def i_end_too(k):
        there = place(k, 2 * (1 - side), 2)
        return cp(TOEND, k, there, there, (dp, jnp.where(is1, 0, 3)))

    def c_agf(k):
        f, d_first, _ = way(k)
        block = g_out.at[2 * k + c, rows(f * HR, HR)]
        return cp(AGF, k, block, block, d_first)

    def c_agc(k):
        block = g_out.at[2 * k + c]
        return cp(AGC, k, block, block, d_core)

    def add(a, b):
        return (a.astype(F32) + b.astype(F32)).astype(B16)

    def produce(k):
        l, r = 0, 0
        for first, across, la, ra in zip(FROM, ACROSS, L_AT, R_AT):
            at = 2 * k - first
            l = jnp.where(at >= 0, la + at // across * BR, l)
            r = jnp.where(at >= 0, ra + at % across * BC, r)
        both = dot(left[:, cols(l, BR)], right[:, cols(r, 2 * BC)], TN).astype(B16)
        for i in range(2):
            part[k % 2, i] = both[:, i * BC:(i + 1) * BC]

    def stage_both(s, k):
        if s == 0:
            produce(k)
            c_core(k).start()
        elif s == 1:
            c_core(k).wait()
            r0[k] = add(r0[k], part[k % 2, c])
            c_first(k).start()

    def stage_flat(s, k):
        f, _, _ = way(k)
        if s == 2:
            c_first(k).wait()
            r1[k] = add(r1[k], r0[k, rows(f * HR, HR)])
            f_second(k).start()
        elif s == 3:
            f_second(k).wait()
            r1[k, own_half(k)] = add(r1[k, own_half(k)], za[k, :2 * SR])

            @pl.when(end)
            def _():
                f_za(k).start()
        elif s == 4:
            @pl.when(mid)
            def _():
                f_za(k).wait_recv()
                r1[k, own_half(k)] = add(r1[k, own_half(k)], zb[k])
                f_zb(k).start()
        elif s == 5:
            @pl.when(mid)
            def _():
                f_zb(k).wait()
                za[k, :2 * SR] = add(r1[k, own_half(k)], zc[k])
                f_zc(k).start()
                f_back(k, False).start()
                f_own(k).start()
        elif s == 6:
            @pl.when(end)
            def _():
                f_zc(k).wait_recv()
                f_back(k, True).start()
                f_za(k).wait_send()
        elif s == 7:
            f_back_in(k).wait_recv()
            f_back(k, True).wait_send()

            @pl.when(mid)
            def _():
                f_own(k).wait()
                f_zc(k).wait_send()
            c_agf(k).start()
        elif s == 8:
            c_agf(k).wait()
            c_agc(k).start()
        elif s == 9:
            c_agc(k).wait()

    def stage_inner(s, k):
        f, _, _ = way(k)
        if s == 2:
            c_first(k).wait()
            r1[k] = add(r1[k], r0[k, rows(f * HR, HR)])

            @pl.when(end)
            def _():
                i_za(k).start()
        elif s == 3:
            @pl.when(mid)
            def _():
                i_za(k).wait_recv()
                r1[k] = add(r1[k], za[k])
                i_zb(k).start()
        elif s == 4:
            @pl.when(mid)
            def _():
                i_zb(k).wait()
                r1[k, mine] = add(r1[k, mine], zb[k])
                i_second(k).start()

            @pl.when(end)
            def _():
                i_za(k).wait_send()
        elif s == 5:
            @pl.when(mid)
            def _():
                i_second(k).wait()
                za[k, :2 * SR] = add(r1[k, mine], zc[k])
                i_mid(k).start()
                i_end(k).start()
                i_own(k).start()
        elif s == 6:
            @pl.when(mid)
            def _():
                i_mid(k).wait()
                i_end_too(k).start()
        elif s == 7:
            @pl.when(mid)
            def _():
                i_own(k).wait()
                i_end(k).wait_send()

            @pl.when(end)
            def _():
                i_end(k).wait_recv()
                i_end_too(k).wait_recv()
            c_agf(k).start()
        elif s == 8:
            c_agf(k).wait()
            c_agc(k).start()

            @pl.when(mid)
            def _():
                i_end_too(k).wait_send()
        elif s == 9:
            c_agc(k).wait()

    steps = ((d_core, None, None), (d_x, None, None), (d_y, None, None),
             ((dp, jnp.where(is0, 1, 2)), end, mid), ((dp, jnp.where(is1, 2, 1)), mid, mid), ((dp, jnp.where(is1, 0, 3)), mid, end))

    def only(cond, f):
        f() if cond is None else pl.when(cond)(f)

    def s_copy(i):
        return pltpu.make_async_remote_copy(src_ref=sm.at[i], dst_ref=smr.at[i], send_sem=smss.at[i], recv_sem=smrs.at[i],
                                            device_id=steps[i][0], device_id_type=MESH)

    def small_step(i):
        if i > 0:
            sm[i] = sm[i - 1]

            def get():
                s_copy(i - 1).wait_recv()
                sm[i] = smr[i - 1] if i == 6 else sm[i - 1] + smr[i - 1]
            only(steps[i - 1][2], get)
        if i < 6:
            only(steps[i][1], lambda: s_copy(i).start())

    def tick(t, _):
        works = {"feed": back_feed, "norm": back_norm, "attend": back_attend, "sums": back_sums, "tokens": back_tokens}
        for phase in range(PHASES):
            def run(stage, s, after, wanted):
                if after % PHASES == phase:
                    k = t - after // PHASES

                    @pl.when(wanted(k))
                    def _():
                        stage(s, k)
            inner = lambda k: (k >= INNER[0]) & (k < INNER[1])
            flat = lambda k: ((k >= 0) & (k < INNER[0])) | ((k >= INNER[1]) & (k < N))
            for s in range(len(OFF) - 1, 1, -1):
                run(stage_flat, s, OFF[s], flat)
                run(stage_inner, s, OFF_INNER[s], inner)
            for s in (1, 0):
                run(stage_both, s, OFF[s], lambda k: (k >= 0) & (k < N))
            for step in range(phase * 2 // PHASES, (phase + 1) * 2 // PHASES):
                for first, count, work in SIDE:
                    @pl.when((t >= first) & (t < first + count))
                    def _():
                        works[work](t - first, step)
        for i in range(7):
            @pl.when(t == SMALL[i])
            def _():
                small_step(i)
        return 0
    lax.fori_loop(0, N + max(OFF[-1], OFF_INNER[-1]) // PHASES, tick, 0)

    small_out[...] = sm[6]
    for i in range(6):
        only(steps[i][1], lambda: s_copy(i).wait_send())
    deal(OUTT, 0).wait()
    for kind in (TOK, LIVE, COT, OUTT):
        finish(kind)
    for m in (1, 2, 3):
        deal(OUTL, m, True).wait_recv()
        deal(OUTT, m, True).wait_recv()


def run_layer(kinds, keeps, *rest):
    tokens = rest[9]
    blocks, BL, _ = tokens.shape
    T = blocks * BL
    V, S, H = (pl.BlockSpec(memory_space=m) for m in (pltpu.VMEM, pltpu.SMEM, pltpu.HBM))
    low16 = lambda *s: pltpu.VMEM(s, B16)
    full = lambda *s: pltpu.VMEM(s, F32)
    sem = lambda *s: pltpu.SemaphoreType.DMA(s)
    return pl.pallas_call(
        layer_kernel,
        out_shape=[jax.ShapeDtypeStruct((2 * N, BR, BC), B16), jax.ShapeDtypeStruct((VECS, D), F32),
                   jax.ShapeDtypeStruct(tokens.shape, B16), jax.ShapeDtypeStruct(tokens.shape, B16)],
        in_specs=[S, S] + [V] * 9 + [H] * 6,
        out_specs=[H, V, H, H],
        scratch_shapes=[
            full(VECS, D), low16(D, 3 * D), low16(D, D), low16(D, FF), low16(FF, D),
            low16(T, L_AT[-1]), low16(T, R_AT[-1]), low16(T, D), pltpu.VMEM((blocks, blocks, BL), jnp.int32), low16(HEADS, T, T),
            full(T, D), full(T, D), low16(T, D),
            low16(T, D), full(T, 1), full(T, T), low16(3, T, HEAD_DIM), full(FF // FB, 1, FB),
            low16(2, 2, BR, BC), low16(N, BR, BC), low16(N, HR, BC), low16(N, HR, BC), low16(N, 2 * SR, BC),
            low16(N, 2 * SR, BC), full(7, VECS, D), full(6, VECS, D),
            sem(KINDS, RING), sem(KINDS, RING), sem(RING), sem(6), sem(6), sem(4), sem(5, 4), sem(5, 4), sem(5),
        ],
        compiler_params=pltpu.CompilerParams(collective_id=0, has_side_effects=True, vmem_limit_bytes=63 * 2**20),
        name="layer",
    )(kinds, keeps, *rest)


AHEAD = 4


def widen_kernel(g, small, out_l, out_t, layer_out, tokens_grad, projection, proj_bias, mixing, mix_bias, attn_gain, attn_shift,
                 expand, expand_bias, contract, contract_bias, ffn_gain, ffn_shift, low, wide, tin, tout, lin, isem, osem, tsem):
    def come(k):
        return pltpu.make_async_copy(g.at[pl.ds(2 * k, 2)], low.at[k], isem.at[k])

    def go(k, ref, at, across):
        return pltpu.make_async_copy(wide.at[k], ref.at[rows(at // across * BR, BR), cols(at % across * 2 * BC, 2 * BC)], osem.at[k])

    t_in, t_out = pltpu.make_async_copy(out_t, tin, tsem.at[0]), pltpu.make_async_copy(tout, tokens_grad, tsem.at[1])
    l_in, l_out = pltpu.make_async_copy(out_l, lin, tsem.at[2]), pltpu.make_async_copy(lin, layer_out, tsem.at[3])
    t_in.start()
    l_in.start()
    for k in range(AHEAD):
        come(k).start()
    grads = list(zip((contract, expand, mixing, projection), FROM, FROM[1:], ACROSS))
    for ref, first, last, across in grads:
        def step(k, _):
            @pl.when(k + AHEAD < N)
            def _():
                come(k + AHEAD).start()
            come(k).wait()
            for i in range(2):
                wide[k, :, i * BC:(i + 1) * BC] = low[k, i].astype(F32)
            go(k, ref, k - first // 2, across // 2).start()
            return 0
        lax.fori_loop(first // 2, last // 2, step, 0)
    l_in.wait()
    l_out.start()
    t_in.wait()
    tout[...] = tin[...].astype(F32)
    t_out.start()
    proj_bias[...] = small[0:2]
    for i, ref in ((2, mix_bias), (3, attn_gain), (4, attn_shift), (9, contract_bias), (10, ffn_gain), (11, ffn_shift)):
        ref[...] = small[i:i + 1].reshape(D)
    for q in range(FF // D):
        expand_bias[q * D:(q + 1) * D] = small[5 + q:6 + q].reshape(D)
    l_out.wait()
    t_out.wait()
    for ref, first, last, across in grads:
        def done(k, _):
            go(k, ref, k - first // 2, across // 2).wait()
            return 0
        lax.fori_loop(first // 2, last // 2, done, 0)


def widen(g, small, out_l, out_t):
    V, H = (pl.BlockSpec(memory_space=m) for m in (pltpu.VMEM, pltpu.HBM))
    shape = lambda *s: jax.ShapeDtypeStruct(s, F32)
    vec = shape(D)
    return pl.pallas_call(
        widen_kernel,
        in_specs=[H, V, H, H],
        out_specs=[H, H, H, V, H, V, V, V, H, V, H, V, V, V],
        out_shape=[jax.ShapeDtypeStruct(out_l.shape, B16), shape(*out_t.shape), shape(D, 3 * D), shape(2, D), shape(D, D),
                   vec, vec, vec, shape(D, FF), shape(FF), shape(FF, D), vec, vec, vec],
        scratch_shapes=[pltpu.VMEM((N, 2, BR, BC), B16), pltpu.VMEM((N, BR, 2 * BC), F32), pltpu.VMEM(out_t.shape, B16),
                        pltpu.VMEM(out_t.shape, F32), pltpu.VMEM(out_l.shape, B16)] + [pltpu.SemaphoreType.DMA((n,)) for n in (N, N, 4)],
        compiler_params=pltpu.CompilerParams(vmem_limit_bytes=60 * 2**20),
        cost_estimate=pl.CostEstimate(flops=0, bytes_accessed=12 * N * BR * BC, transcendentals=0),
        name="widen",
    )(g, small, out_l, out_t)


def local(tokens, row_kinds, live_mask, keep_flag, projection, proj_bias, mixing, mix_bias, attn_gain, attn_shift,
          expand, expand_bias, contract, contract_bias, ffn_gain, ffn_shift, cotangent):
    g, small, layer_out, tokens_grad = run_layer(
        row_kinds, keep_flag, proj_bias, mix_bias, attn_gain, attn_shift, expand_bias, contract_bias, ffn_gain, ffn_shift,
        live_mask, tokens, cotangent, projection, mixing, expand, contract)
    groups = lax.axis_size("dp") // 8
    if groups > 1:
        index = [[i + 8 * j for j in range(groups)] for i in range(8)]
        g, small = lax.psum((g, small), "dp", axis_index_groups=index)
    return tuple(widen(g, small, layer_out, tokens_grad))


def solution(mesh):
    data = P("dp", "blk", None)
    in_specs = (data, P("dp"), P("dp", "blk"), P("dp")) + (P(),) * 12 + (data,)
    out_specs = (data, data) + (P(),) * 12
    return jax.shard_map(local, mesh=mesh, in_specs=in_specs, out_specs=out_specs, check_vma=False)
```

```python
import functools

import jax
import jax.numpy as jnp
from jax import lax
from jax.experimental import pallas as pl
from jax.experimental.pallas import tpu as pltpu
from jax.sharding import PartitionSpec as P

D = 768
FF = 3072
HEADS = 12
HEAD_DIM = 64
DOC_SHORT = 128
MESH = pl.DeviceIdType.MESH
EPS = 1e-05
NEG = -1e9
F32, B16 = jnp.float32, jnp.bfloat16
NN = (((1,), (0,)), ((), ()))
NT = (((1,), (1,)), ((), ()))
TN = (((0,), (0,)), ((), ()))

FB = 512
BR, BC = 384, 384
HR = BR // 2
SR = HR // 4
ACROSS = (D // BC, FF // BC, D // BC, 3 * D // BC)
DOWN = (FF // BR, D // BR, D // BR, D // BR)
FROM = [0]
for _down, _across in zip(DOWN, ACROSS):
    FROM.append(FROM[-1] + _down * _across)
N = FROM[-1] // 2
L_AT = (0, FF, FF + D, FF + 2 * D, FF + 3 * D)
R_AT = (0, D, D + FF, 2 * D + FF, 5 * D + FF)
KINDS = 15
CORE, FIRST, SECOND, ZA, ZB, ZC, BACK, AGF, AGC, MID, TOEND, I_ZA, I_ZB, I_ZC, I_SECOND = range(KINDS)
INNER = (10, 18)
RING = 8
PHASES = 2
OFF = [0, 2, 8, 12, 16, 20, 24, 28, 34, 38]
OFF_INNER = [0, 2, 8, 13, 17, 21, 25, 29, 35, 39]
SMALL = [18 + 4 * i for i in range(7)]
SIDE = ((0, 6, "feed"), (7, 1, "norm"), (9, 6, "attend"), (15, 1, "sums"), (16, 4, "tokens"))
VECS = 16


def dot(a, b, dims=NN):
    return lax.dot_general(a, b, dims, preferred_element_type=F32)


def rows(start, n):
    return pl.ds(pl.multiple_of(start, 16), n)


def cols(start, n):
    return pl.ds(pl.multiple_of(start, 128), n)


def normal_parts(v):
    t = 1.0 / (1.0 + (0.3275911 * 0.5 ** 0.5) * jnp.abs(v))
    ex = jnp.exp(-0.5 * (v * v))
    poly = t * (0.127414796 + t * (-0.142248368 + t * (0.7107068705 + t * (-0.7265760135 + t * 0.5307027145))))
    tail = poly * ex
    below = jnp.where(v < 0, tail, 1.0 - tail)
    return v * below, below + v * (ex * 0.3989422804014327)


def mean(a):
    return jnp.sum(a, axis=1, keepdims=True) * (1.0 / D)


def layer_kernel(kinds, keeps, proj_bias, mix_bias, attn_gain, attn_shift, expand_bias, contract_bias, ffn_gain, ffn_shift,
                 live, tokens, cot_in, w_proj, w_mix, w_exp, w_con,
                 g_out, small_out, out_l, out_t,
                 vecs, wproj, wmix, wexp, wcon, left, right, cot, livebuf, probs, xhat, dres, d_att,
                 send, rstd, bias, held, ebuf,
                 part, r0, r1, za, zb, zc, sm, smr,
                 ssem, rsem, lsem, smss, smrs, wsem, dsend, drecv, dloc):
    dp, z = lax.axis_index("dp"), lax.axis_index("blk")
    T = left.shape[0]
    act, low, att, row = (left.at[:, a:b] for a, b in zip(L_AT, L_AT[1:]))
    d_ffn, gp, d_attn, qkv = (right.at[:, a:b] for a, b in zip(R_AT, R_AT[1:]))
    BL = T // 4
    c, x, y = dp % 2, (dp // 2) % 2, (dp // 4) % 2
    d_core = (dp + 1 - 2 * c, z)
    d_x = (dp + 2 - 4 * x, z)
    d_y = (dp + 4 - 8 * y, z)
    is0, is1 = z == 0, z == 1
    end, mid = (z == 0) | (z == 3), (z == 1) | (z == 2)
    others = (z, z + 1 - 2 * (z % 2), z + 2 - 4 * (z // 2), 3 - z)

    loads = [pltpu.make_async_copy(a, b, wsem.at[i]) for i, (a, b) in
             enumerate(((w_proj, wproj), (w_mix, wmix), (w_exp, wexp), (w_con, wcon)))]

    barrier = pltpu.get_barrier_semaphore()
    for d in (d_core, d_x, d_y) + tuple((dp, others[m]) for m in (1, 2, 3)):
        pl.semaphore_signal(barrier, inc=1, device_id=d, device_id_type=MESH)
    pl.semaphore_wait(barrier, 6)

    TOK, LIVE, COT, OUTL, OUTT = range(5)

    def deal(kind, m, arriving=False):
        there = others[m]
        src, dst = {
            TOK: lambda: (tokens.at[there], row.at[rows((there if arriving else z) * BL, BL)]),
            LIVE: lambda: (live, livebuf.at[there if arriving else z]),
            COT: lambda: (cot_in.at[there], cot.at[rows((there if arriving else z) * BL, BL)]),
            OUTL: lambda: (send.at[rows(there * BL, BL)], out_l.at[there if arriving else z]),
            OUTT: lambda: (send.at[rows(there * BL, BL)], out_t.at[there if arriving else z]),
        }[kind]()
        if m == 0:
            return pltpu.make_async_copy(src, dst, dloc.at[kind])
        return pltpu.make_async_remote_copy(src_ref=src, dst_ref=dst, send_sem=dsend.at[kind, m], recv_sem=drecv.at[kind, m],
                                            device_id=(dp, there), device_id_type=MESH)

    def finish(kind):
        for m in (1, 2, 3):
            deal(kind, m).wait_send()

    for m in (3, 2, 1, 0):
        deal(LIVE, m).start()
        deal(TOK, m).start()
    for load in loads:
        load.start()
    wide = lambda v: v[...].astype(F32).reshape(1, v.shape[0])
    vecs[0:1] = proj_bias[0:1].astype(F32)
    vecs[1:2] = jnp.zeros((1, D), F32)
    vecs[2:3] = proj_bias[1:2].astype(F32)
    for i, v in enumerate((mix_bias, attn_gain, attn_shift, contract_bias, ffn_gain, ffn_shift)):
        vecs[3 + i:4 + i] = wide(v)
    ebias = wide(expand_bias)
    for j in range(FF // FB):
        ebuf[j] = ebias[:, j * FB:(j + 1) * FB]

    def project(m):
        (deal(TOK, 0).wait if m == 0 else deal(TOK, m, True).wait_recv)()
        r = rows(others[m] * BL, BL)
        for j in range(3):
            s = slice(j * D, (j + 1) * D)
            part_j = dot(row[r], wproj[:, s]) + vecs[j:j + 1]
            if j == 0:
                part_j = part_j.astype(B16).astype(F32) * HEAD_DIM ** -0.5
            qkv[r, s] = part_j.astype(B16)

    loads[0].wait()
    for m in (0, 1, 2, 3):
        project(m)
    for m in (3, 2, 1, 0):
        deal(COT, m).start()

    deal(LIVE, 0).wait()
    for m in (1, 2, 3):
        deal(LIVE, m, True).wait_recv()
    count = jnp.sum(sum(livebuf[j, pl.ds(z, 1)] for j in range(4)), axis=1, keepdims=True)
    short = (1 - kinds[z]).astype(F32) * NEG
    for b in range(4):
        key = lax.broadcasted_iota(jnp.int32, (BL, T), 0) + b * BL
        query = lax.broadcasted_iota(jnp.int32, (BL, T), 1)
        shift = DOC_SHORT.bit_length() - 1
        apart = jnp.where((key >> shift) == (query >> shift), 0.0, short)
        bias[b * BL:(b + 1) * BL] = jnp.where(key < count, apart, NEG)

    def attend_pair(i):
        s = cols(i * 2 * HEAD_DIM, 2 * HEAD_DIM)
        q2, k2, v2 = (qkv[:, cols(j * D + i * 2 * HEAD_DIM, 2 * HEAD_DIM)] for j in range(3))
        outs = []
        for h in range(2):
            hs = slice(h * HEAD_DIM, (h + 1) * HEAD_DIM)
            scores = dot(k2[:, hs], q2[:, hs], NT) + bias[...]
            e = jnp.exp(scores - jnp.max(scores, axis=0, keepdims=True))
            p = (e * (1.0 / jnp.sum(e, axis=0, keepdims=True))).astype(B16)
            probs[2 * i + h] = p
            outs.append(dot(v2[:, hs], p, TN))
        att[:, s] = jnp.concatenate(outs, axis=0).T.astype(B16)
    def attend(i, _):
        for j in range(2):
            attend_pair(i * 2 + j)
        return 0
    lax.fori_loop(0, HEADS // 4, attend, 0)

    loads[1].wait()
    RB = 256

    def norm_one(i, _):
        r = rows(i * RB, RB)
        h = row[r].astype(F32) + (dot(att[r], wmix[...]) + vecs[3:4])
        h = h - mean(h)
        rs = lax.rsqrt(mean(h * h) + EPS)
        h = h * rs
        xhat[r] = h
        rstd[r] = rs
        low[r] = (h * vecs[4:5] + vecs[5:6]).astype(B16)
        return 0
    lax.fori_loop(0, T // RB, norm_one, 0)

    loads[2].wait()
    loads[3].wait()
    dres[...] = jnp.zeros_like(dres)

    def feed(j, _):
        s = cols(j * FB, FB)
        parts = [slice(i * T // 2, (i + 1) * T // 2) for i in range(2)]
        pres = [dot(low[p, :], wexp[:, s]) + ebuf[j] for p in parts]
        for p, pre in zip(parts, pres):
            value, slope = normal_parts(pre)
            value = value.astype(B16)
            act[p, s] = value
            gp[p, s] = slope.astype(B16)
            dres[p, :] += dot(value, wcon[rows(j * FB, FB)])
        return 0
    lax.fori_loop(0, FF // FB, feed, 0)

    keep = keeps[z].astype(F32)
    for kind in (COT,):
        deal(kind, 0).wait()
        for m in (1, 2, 3):
            deal(kind, m, True).wait_recv()
    sm[0] = jnp.zeros((VECS, D), F32)

    def norm_two(i, _):
        r = rows(i * BL, BL)
        h = (xhat[r] * vecs[4:5] + vecs[5:6]) + (dres[r] + vecs[6:7])
        h = h - mean(h)
        rs = lax.rsqrt(mean(h * h) + EPS)
        h = h * rs
        send[r] = jnp.where(keep > 0, h * vecs[7:8] + vecs[8:9], row[r].astype(F32)).astype(B16)
        grad = cot[r].astype(F32) * keep
        sm[0, 10:11] += jnp.sum(grad * h, axis=0, keepdims=True)
        sm[0, 11:12] += jnp.sum(grad, axis=0, keepdims=True)
        dx = grad * vecs[7:8]
        dr = rs * (dx - mean(dx) - h * mean(dx * h))
        dres[r] = dr
        dr = dr.astype(B16)
        d_ffn[r] = dr
        sm[0, 9:10] += jnp.sum(dr.astype(F32), axis=0, keepdims=True)
        return 0
    lax.fori_loop(0, T // BL, norm_two, 0)
    for m in (3, 2, 1, 0):
        deal(OUTL, m).start()

    def back_feed(j, step):
        s = cols(j * FB, FB)
        if step == 0:
            gp[:, s] = (dot(d_ffn[...], wcon[rows(j * FB, FB)], NT) * gp[:, s].astype(F32)).astype(B16)
        else:
            dres[...] += dot(gp[:, s], wexp[:, s], NT)

    def back_norm(_, step):
        if step == 1:
            d_att[...] = dot(d_attn[...], wmix[...], NT).astype(B16)
            return
        for q in range(FF // D):
            sm[0, 5 + q:6 + q] = jnp.sum(gp[:, q * D:(q + 1) * D].astype(F32), axis=0, keepdims=True)

        def block(i, _):
            r = rows(i * BL, BL)
            dn, h = dres[r], xhat[r]
            sm[0, 3:4] += jnp.sum(dn * h, axis=0, keepdims=True)
            sm[0, 4:5] += jnp.sum(dn, axis=0, keepdims=True)
            dx = dn * vecs[4:5]
            dr = rstd[r] * (dx - mean(dx) - h * mean(dx * h))
            dres[r] = dr
            dr = dr.astype(B16)
            d_attn[r] = dr
            sm[0, 2:3] += jnp.sum(dr.astype(F32), axis=0, keepdims=True)
            return 0
        lax.fori_loop(0, T // BL, block, 0)

    def back_attend(i, step):
        at = [cols(j * D + i * 2 * HEAD_DIM, 2 * HEAD_DIM) for j in range(3)]
        hs = slice(step * HEAD_DIM, (step + 1) * HEAD_DIM)
        q1, k1, v1 = (qkv[:, s][:, hs] for s in at)
        da1 = d_att[:, at[0]][:, hs]
        p = probs[2 * i + step]
        dp_t = dot(v1, da1, NT)
        pf = p.astype(F32)
        delta = jnp.sum(pf * dp_t, axis=0, keepdims=True)
        ds = (pf * (dp_t - delta)).astype(B16)
        dq = (dot(k1, ds, TN) * HEAD_DIM ** -0.5).T
        dk, dv = dot(ds, q1), dot(p, da1)
        for j, d in enumerate((dq, dk, dv)):
            if step == 0:
                held[j] = d.astype(B16)
            else:
                qkv[:, at[j]] = jnp.concatenate([held[j], d.astype(B16)], axis=1)

    def back_sums(_, step):
        if step:
            return
        sm[0, 0:1] = jnp.sum(qkv[:, 0:D].astype(F32), axis=0, keepdims=True)
        sm[0, 1:2] = jnp.sum(qkv[:, 2 * D:].astype(F32), axis=0, keepdims=True)

    def back_tokens(i, step):
        for m in range(4) if step == 0 else ():
            @pl.when(i == m)
            def _():
                if m == 0:
                    deal(OUTL, 0).wait()
                    finish(OUTL)
                r = rows(others[m] * BL, BL)
                d = dres[r] + dot(qkv[r], wproj[...], NT)
                send[r] = jnp.where(keep > 0, d, cot[r].astype(F32)).astype(B16)
                deal(OUTT, m).start()

    def cp(kind, k, src, dst, dev):
        return pltpu.make_async_remote_copy(src_ref=src, dst_ref=dst, send_sem=ssem.at[kind, k % RING],
                                            recv_sem=rsem.at[kind, k % RING], device_id=dev, device_id_type=MESH)

    def way(k):
        par = k % 2
        f = x * (1 - par) + y * par
        d_first = (dp + (1 - par) * (2 - 4 * x) + par * (4 - 8 * y), z)
        d_last = (dp + par * (2 - 4 * x) + (1 - par) * (4 - 8 * y), z)
        return f, d_first, d_last

    def c_core(k):
        return cp(CORE, k, part.at[k % 2, 1 - c], r0.at[k], d_core)

    def c_first(k):
        f, d_first, _ = way(k)
        return cp(FIRST, k, r0.at[k, rows((1 - f) * HR, HR)], r1.at[k], d_first)

    def place(k, shard, n=1):
        f, _, _ = way(k)
        return g_out.at[2 * k + c, rows(f * HR + shard * SR, n * SR)]

    def half(k):
        par = k % 2
        return y * (1 - par) + x * par

    def own_half(k):
        return rows(half(k) * 2 * SR, 2 * SR)

    def f_second(k):
        _, _, d_last = way(k)
        return cp(SECOND, k, r1.at[k, rows((1 - half(k)) * 2 * SR, 2 * SR)], za.at[k, rows(0, 2 * SR)], d_last)

    def f_za(k):
        return cp(ZA, k, r1.at[k, own_half(k)], zb.at[k], (dp, jnp.where(is0, 1, 2)))

    def f_zb(k):
        return cp(ZB, k, r1.at[k, own_half(k)], zc.at[k], (dp, jnp.where(is1, 2, 1)))

    def f_place(k):
        return place(k, 2 * half(k), 2)

    def f_zc(k):
        return cp(ZC, k, za.at[k, rows(0, 2 * SR)], f_place(k), (dp, jnp.where(is1, 0, 3)))

    def f_own(k):
        return pltpu.make_async_copy(za.at[k, rows(0, 2 * SR)], f_place(k), lsem.at[k % RING])

    def f_back(k, from_place):
        _, _, d_last = way(k)
        return cp(BACK, k, f_place(k) if from_place else za.at[k, rows(0, 2 * SR)], f_place(k), d_last)

    def f_back_in(k):
        _, _, d_last = way(k)
        there = place(k, 2 * (1 - half(k)), 2)
        return cp(BACK, k, there, there, d_last)

    side = jnp.where(z < 2, 0, 1)
    mine, theirs = rows(side * 2 * SR, 2 * SR), rows((1 - side) * 2 * SR, 2 * SR)

    def i_za(k):
        return cp(I_ZA, k, r1.at[k], za.at[k], (dp, jnp.where(is0, 1, 2)))

    def i_zb(k):
        return cp(I_ZB, k, r1.at[k, theirs], zb.at[k], (dp, jnp.where(is1, 2, 1)))

    def i_second(k):
        _, _, d_last = way(k)
        return cp(I_SECOND, k, r1.at[k, mine], zc.at[k], d_last)

    def i_own(k):
        return pltpu.make_async_copy(za.at[k, rows(0, 2 * SR)], place(k, 2 * side, 2), lsem.at[k % RING])

    def i_mid(k):
        return cp(MID, k, za.at[k, rows(0, 2 * SR)], place(k, 2 * side, 2), (dp, jnp.where(is1, 2, 1)))

    def i_end(k):
        return cp(I_ZC, k, za.at[k, rows(0, 2 * SR)], place(k, 2 * side, 2), (dp, jnp.where(is1, 0, 3)))

    def i_end_too(k):
        there = place(k, 2 * (1 - side), 2)
        return cp(TOEND, k, there, there, (dp, jnp.where(is1, 0, 3)))

    def c_agf(k):
        f, d_first, _ = way(k)
        block = g_out.at[2 * k + c, rows(f * HR, HR)]
        return cp(AGF, k, block, block, d_first)

    def c_agc(k):
        block = g_out.at[2 * k + c]
        return cp(AGC, k, block, block, d_core)

    def add(a, b):
        return (a.astype(F32) + b.astype(F32)).astype(B16)

    def produce(k):
        l, r = 0, 0
        for first, across, la, ra in zip(FROM, ACROSS, L_AT, R_AT):
            at = 2 * k - first
            l = jnp.where(at >= 0, la + at // across * BR, l)
            r = jnp.where(at >= 0, ra + at % across * BC, r)
        both = dot(left[:, cols(l, BR)], right[:, cols(r, 2 * BC)], TN).astype(B16)
        for i in range(2):
            part[k % 2, i] = both[:, i * BC:(i + 1) * BC]

    def stage_both(s, k):
        if s == 0:
            produce(k)
            c_core(k).start()
        elif s == 1:
            c_core(k).wait()
            r0[k] = add(r0[k], part[k % 2, c])
            c_first(k).start()

    def stage_flat(s, k):
        f, _, _ = way(k)
        if s == 2:
            c_first(k).wait()
            r1[k] = add(r1[k], r0[k, rows(f * HR, HR)])
            f_second(k).start()
        elif s == 3:
            f_second(k).wait()
            r1[k, own_half(k)] = add(r1[k, own_half(k)], za[k, :2 * SR])

            @pl.when(end)
            def _():
                f_za(k).start()
        elif s == 4:
            @pl.when(mid)
            def _():
                f_za(k).wait_recv()
                r1[k, own_half(k)] = add(r1[k, own_half(k)], zb[k])
                f_zb(k).start()
        elif s == 5:
            @pl.when(mid)
            def _():
                f_zb(k).wait()
                za[k, :2 * SR] = add(r1[k, own_half(k)], zc[k])
                f_zc(k).start()
                f_back(k, False).start()
                f_own(k).start()
        elif s == 6:
            @pl.when(end)
            def _():
                f_zc(k).wait_recv()
                f_back(k, True).start()
                f_za(k).wait_send()
        elif s == 7:
            f_back_in(k).wait_recv()
            f_back(k, True).wait_send()

            @pl.when(mid)
            def _():
                f_own(k).wait()
                f_zc(k).wait_send()
            c_agf(k).start()
        elif s == 8:
            c_agf(k).wait()
            c_agc(k).start()
        elif s == 9:
            c_agc(k).wait()

    def stage_inner(s, k):
        f, _, _ = way(k)
        if s == 2:
            c_first(k).wait()
            r1[k] = add(r1[k], r0[k, rows(f * HR, HR)])

            @pl.when(end)
            def _():
                i_za(k).start()
        elif s == 3:
            @pl.when(mid)
            def _():
                i_za(k).wait_recv()
                r1[k] = add(r1[k], za[k])
                i_zb(k).start()
        elif s == 4:
            @pl.when(mid)
            def _():
                i_zb(k).wait()
                r1[k, mine] = add(r1[k, mine], zb[k])
                i_second(k).start()

            @pl.when(end)
            def _():
                i_za(k).wait_send()
        elif s == 5:
            @pl.when(mid)
            def _():
                i_second(k).wait()
                za[k, :2 * SR] = add(r1[k, mine], zc[k])
                i_mid(k).start()
                i_end(k).start()
                i_own(k).start()
        elif s == 6:
            @pl.when(mid)
            def _():
                i_mid(k).wait()
                i_end_too(k).start()
        elif s == 7:
            @pl.when(mid)
            def _():
                i_own(k).wait()
                i_end(k).wait_send()

            @pl.when(end)
            def _():
                i_end(k).wait_recv()
                i_end_too(k).wait_recv()
            c_agf(k).start()
        elif s == 8:
            c_agf(k).wait()
            c_agc(k).start()

            @pl.when(mid)
            def _():
                i_end_too(k).wait_send()
        elif s == 9:
            c_agc(k).wait()

    steps = ((d_core, None, None), (d_x, None, None), (d_y, None, None),
             ((dp, jnp.where(is0, 1, 2)), end, mid), ((dp, jnp.where(is1, 2, 1)), mid, mid), ((dp, jnp.where(is1, 0, 3)), mid, end))

    def only(cond, f):
        f() if cond is None else pl.when(cond)(f)

    def s_copy(i):
        return pltpu.make_async_remote_copy(src_ref=sm.at[i], dst_ref=smr.at[i], send_sem=smss.at[i], recv_sem=smrs.at[i],
                                            device_id=steps[i][0], device_id_type=MESH)

    def small_step(i):
        if i > 0:
            sm[i] = sm[i - 1]

            def get():
                s_copy(i - 1).wait_recv()
                sm[i] = smr[i - 1] if i == 6 else sm[i - 1] + smr[i - 1]
            only(steps[i - 1][2], get)
        if i < 6:
            only(steps[i][1], lambda: s_copy(i).start())

    def tick(t, _):
        works = {"feed": back_feed, "norm": back_norm, "attend": back_attend, "sums": back_sums, "tokens": back_tokens}
        for phase in range(PHASES):
            def run(stage, s, after, wanted):
                if after % PHASES == phase:
                    k = t - after // PHASES

                    @pl.when(wanted(k))
                    def _():
                        stage(s, k)
            inner = lambda k: (k >= INNER[0]) & (k < INNER[1])
            flat = lambda k: ((k >= 0) & (k < INNER[0])) | ((k >= INNER[1]) & (k < N))
            for s in range(len(OFF) - 1, 1, -1):
                run(stage_flat, s, OFF[s], flat)
                run(stage_inner, s, OFF_INNER[s], inner)
            for s in (1, 0):
                run(stage_both, s, OFF[s], lambda k: (k >= 0) & (k < N))
            for step in range(phase * 2 // PHASES, (phase + 1) * 2 // PHASES):
                for first, count, work in SIDE:
                    @pl.when((t >= first) & (t < first + count))
                    def _():
                        works[work](t - first, step)
        for i in range(7):
            @pl.when(t == SMALL[i])
            def _():
                small_step(i)
        return 0
    lax.fori_loop(0, N + max(OFF[-1], OFF_INNER[-1]) // PHASES, tick, 0)

    small_out[...] = sm[6]
    for i in range(6):
        only(steps[i][1], lambda: s_copy(i).wait_send())
    deal(OUTT, 0).wait()
    for kind in (TOK, LIVE, COT, OUTT):
        finish(kind)
    for m in (1, 2, 3):
        deal(OUTL, m, True).wait_recv()
        deal(OUTT, m, True).wait_recv()


def run_layer(kinds, keeps, *rest):
    tokens = rest[9]
    blocks, BL, _ = tokens.shape
    T = blocks * BL
    V, S, H = (pl.BlockSpec(memory_space=m) for m in (pltpu.VMEM, pltpu.SMEM, pltpu.HBM))
    low16 = lambda *s: pltpu.VMEM(s, B16)
    full = lambda *s: pltpu.VMEM(s, F32)
    sem = lambda *s: pltpu.SemaphoreType.DMA(s)
    return pl.pallas_call(
        layer_kernel,
        out_shape=[jax.ShapeDtypeStruct((2 * N, BR, BC), B16), jax.ShapeDtypeStruct((VECS, D), F32),
                   jax.ShapeDtypeStruct(tokens.shape, B16), jax.ShapeDtypeStruct(tokens.shape, B16)],
        in_specs=[S, S] + [V] * 9 + [H] * 6,
        out_specs=[H, V, H, H],
        scratch_shapes=[
            full(VECS, D), low16(D, 3 * D), low16(D, D), low16(D, FF), low16(FF, D),
            low16(T, L_AT[-1]), low16(T, R_AT[-1]), low16(T, D), pltpu.VMEM((blocks, blocks, BL), jnp.int32), low16(HEADS, T, T),
            full(T, D), full(T, D), low16(T, D),
            low16(T, D), full(T, 1), full(T, T), low16(3, T, HEAD_DIM), full(FF // FB, 1, FB),
            low16(2, 2, BR, BC), low16(N, BR, BC), low16(N, HR, BC), low16(N, HR, BC), low16(N, 2 * SR, BC),
            low16(N, 2 * SR, BC), full(7, VECS, D), full(6, VECS, D),
            sem(KINDS, RING), sem(KINDS, RING), sem(RING), sem(6), sem(6), sem(4), sem(5, 4), sem(5, 4), sem(5),
        ],
        compiler_params=pltpu.CompilerParams(collective_id=0, has_side_effects=True, vmem_limit_bytes=63 * 2**20),
        name="layer",
    )(kinds, keeps, *rest)


AHEAD = 4


def widen_kernel(g, small, out_l, out_t, layer_out, tokens_grad, projection, proj_bias, mixing, mix_bias, attn_gain, attn_shift,
                 expand, expand_bias, contract, contract_bias, ffn_gain, ffn_shift, low, wide, tin, tout, lin, isem, osem, tsem):
    def come(k):
        return pltpu.make_async_copy(g.at[pl.ds(2 * k, 2)], low.at[k], isem.at[k])

    def go(k, ref, at, across):
        return pltpu.make_async_copy(wide.at[k], ref.at[rows(at // across * BR, BR), cols(at % across * 2 * BC, 2 * BC)], osem.at[k])

    t_in, t_out = pltpu.make_async_copy(out_t, tin, tsem.at[0]), pltpu.make_async_copy(tout, tokens_grad, tsem.at[1])
    l_in, l_out = pltpu.make_async_copy(out_l, lin, tsem.at[2]), pltpu.make_async_copy(lin, layer_out, tsem.at[3])
    t_in.start()
    l_in.start()
    for k in range(AHEAD):
        come(k).start()
    grads = list(zip((contract, expand, mixing, projection), FROM, FROM[1:], ACROSS))
    for ref, first, last, across in grads:
        def step(k, _):
            @pl.when(k + AHEAD < N)
            def _():
                come(k + AHEAD).start()
            come(k).wait()
            for i in range(2):
                wide[k, :, i * BC:(i + 1) * BC] = low[k, i].astype(F32)
            go(k, ref, k - first // 2, across // 2).start()
            return 0
        lax.fori_loop(first // 2, last // 2, step, 0)
    l_in.wait()
    l_out.start()
    t_in.wait()
    tout[...] = tin[...].astype(F32)
    t_out.start()
    proj_bias[...] = small[0:2]
    for i, ref in ((2, mix_bias), (3, attn_gain), (4, attn_shift), (9, contract_bias), (10, ffn_gain), (11, ffn_shift)):
        ref[...] = small[i:i + 1].reshape(D)
    for q in range(FF // D):
        expand_bias[q * D:(q + 1) * D] = small[5 + q:6 + q].reshape(D)
    l_out.wait()
    t_out.wait()
    for ref, first, last, across in grads:
        def done(k, _):
            go(k, ref, k - first // 2, across // 2).wait()
            return 0
        lax.fori_loop(first // 2, last // 2, done, 0)


def widen(g, small, out_l, out_t):
    V, H = (pl.BlockSpec(memory_space=m) for m in (pltpu.VMEM, pltpu.HBM))
    shape = lambda *s: jax.ShapeDtypeStruct(s, F32)
    vec = shape(D)
    return pl.pallas_call(
        widen_kernel,
        in_specs=[H, V, H, H],
        out_specs=[H, H, H, V, H, V, V, V, H, V, H, V, V, V],
        out_shape=[jax.ShapeDtypeStruct(out_l.shape, B16), shape(*out_t.shape), shape(D, 3 * D), shape(2, D), shape(D, D),
                   vec, vec, vec, shape(D, FF), shape(FF), shape(FF, D), vec, vec, vec],
        scratch_shapes=[pltpu.VMEM((N, 2, BR, BC), B16), pltpu.VMEM((N, BR, 2 * BC), F32), pltpu.VMEM(out_t.shape, B16),
                        pltpu.VMEM(out_t.shape, F32), pltpu.VMEM(out_l.shape, B16)] + [pltpu.SemaphoreType.DMA((n,)) for n in (N, N, 4)],
        compiler_params=pltpu.CompilerParams(vmem_limit_bytes=60 * 2**20),
        cost_estimate=pl.CostEstimate(flops=0, bytes_accessed=12 * N * BR * BC, transcendentals=0),
        name="widen",
    )(g, small, out_l, out_t)


def local(tokens, row_kinds, live_mask, keep_flag, projection, proj_bias, mixing, mix_bias, attn_gain, attn_shift,
          expand, expand_bias, contract, contract_bias, ffn_gain, ffn_shift, cotangent):
    g, small, layer_out, tokens_grad = run_layer(
        row_kinds, keep_flag, proj_bias, mix_bias, attn_gain, attn_shift, expand_bias, contract_bias, ffn_gain, ffn_shift,
        live_mask, tokens, cotangent, projection, mixing, expand, contract)
    groups = lax.axis_size("dp") // 8
    if groups > 1:
        index = [[i + 8 * j for j in range(groups)] for i in range(8)]
        g, small = lax.psum((g, small), "dp", axis_index_groups=index)
    return tuple(widen(g, small, layer_out, tokens_grad))


def solution(mesh):
    data = P("dp", "blk", None)
    in_specs = (data, P("dp"), P("dp", "blk"), P("dp")) + (P(),) * 12 + (data,)
    out_specs = (data, data) + (P(),) * 12
    return jax.shard_map(local, mesh=mesh, in_specs=in_specs, out_specs=out_specs, check_vma=False)
```
